128 devices in a mesh: morton: 32 (over z, y, core), lane: 4 (over x).
Axes of the slice: x: 4, y: 4, z: 4, core: 2. Of those that a mesh axis runs over, the one named last changes fastest.
Arguments:
- cons_old: float32 [4096, 8, 4096], P(('morton', 'lane')), may hold values from -6 to 6
- flagged: int32 [256], replicated, may hold values from 0 to 4095, as said below
- new_owner: int32 [256], replicated, may hold values from 0 to 127, as said below
- diffusivity: float32 [8], replicated, may hold values from 0.02 to 0.1
- courant: float32 [8], replicated, may hold values from 0.05 to 0.3
Outputs:
- coarse_next: float32 [4096, 8, 4096], P(('morton', 'lane'))
- children: float32 [384, 8, 8, 4096], P(('morton', 'lane'))
The draws below stay inside these ranges and needn't reach their ends.
Inputs may be any that keep to these rules, and one draw needn't show every extreme that they name: `flagged`: Strictly increasing. The 32 meshblocks of one device hold 0 to 4 flagged parents, some device exactly 4. `new_owner`: Nondecreasing. Each device receives the children of 1 to 3 parents, some device exactly 3. A parent's new owner differs from the device that holds it (flagged // 32) by at most 2, and by exactly 2 in either direction for some parent.
All inputs are finite; a program needn't handle non-finite values.
Results may differ from the reference program's by a relative error of at most 0.000052.
Values sent between devices are 32-bit elements; how exact they have to be, the bound alone decides.
No kernel may reach another device: no remote copies, remote signals or barrier semaphores. Data moves between devices by JAX's collectives and lax.ppermute only.
A program may use at most 192 MiB of HBM per device.

```python
import math
import jax
import jax.numpy as jnp
from jax import lax

EDGE = 16
NF = 8
OLD_DEV = 32
PAR_DEV = 2
CAP = 3
CELLS = 4096
BLOCKS = 4096
PARENTS = 256
SLOTS = 384


def forced_pairs(key):
    devices = PARENTS // PAR_DEV
    pairs = devices // 2
    first_pair = jax.random.randint(jax.random.fold_in(key, 101), (), 0, pairs // 2 - 1)
    second_pair = jax.random.randint(jax.random.fold_in(key, 102), (), pairs // 2 + 1, pairs)
    return (first_pair, second_pair)


def owners_from(counts, number):
    starts = jnp.cumsum(counts) - counts
    places = jnp.arange(number, dtype=jnp.int32)
    owner = jnp.sum((starts[None, :] <= places[:, None]).astype(jnp.int32), axis=1) - 1
    return (owner.astype(jnp.int32), starts)


def draw_flagged(key, part):
    first_pair, second_pair = forced_pairs(key)
    key = jax.random.fold_in(key, 3)
    devices = PARENTS // PAR_DEV
    pairs = devices // 2
    kinds = jax.random.randint(jax.random.fold_in(key, 1), (pairs,), 0, 3)
    kinds = kinds.at[first_pair].set(1).at[second_pair].set(2)
    leading = jnp.where(kinds == 0, PAR_DEV, jnp.where(kinds == 1, 2 * PAR_DEV, 0))
    counts = jnp.stack([leading, 2 * PAR_DEV - leading], axis=1).reshape(devices).astype(jnp.int32)
    owner, starts = owners_from(counts, PARENTS)
    device_keys = jax.random.split(jax.random.fold_in(key, 2), devices)
    shuffled = jax.vmap(lambda single: jax.random.permutation(single, OLD_DEV))(device_keys)
    chosen = jnp.sort(shuffled[:, :2 * PAR_DEV], axis=1)
    within = jnp.arange(PARENTS, dtype=jnp.int32) - starts[owner]
    local_idx = chosen[owner, within]
    return (owner * OLD_DEV + local_idx).astype(jnp.int32)


def draw_new_owner(key, part):
    first_pair, second_pair = forced_pairs(key)
    key = jax.random.fold_in(key, 4)
    devices = PARENTS // PAR_DEV
    pairs = devices // 2
    kinds = jax.random.randint(jax.random.fold_in(key, 1), (pairs - 1,), 0, 3)
    kinds = kinds.at[first_pair].set(2).at[second_pair - 1].set(1)
    leading = jnp.where(kinds == 0, PAR_DEV, jnp.where(kinds == 1, PAR_DEV + 1, PAR_DEV - 1))
    inner = jnp.stack([leading, 2 * PAR_DEV - leading], axis=1).reshape(devices - 2)
    edges_count = jnp.full((1,), PAR_DEV, dtype=jnp.int32)
    counts = jnp.concatenate([edges_count, inner.astype(jnp.int32), edges_count])
    owner, starts = owners_from(counts, PARENTS)
    return owner


def block_scale(rng, shape, cuts, low, high):
    factor_of = 1.0
    for position, blocks in cuts:
        heights = jax.random.uniform(jax.random.fold_in(jax.random.fold_in(rng, 6), position), (blocks,), jnp.float32, low / len(cuts), high / len(cuts))
        factor_of = factor_of * jnp.repeat(jnp.exp(heights), shape[position] // blocks).reshape((-1,) + (1,) * (len(shape) - 1 - position))
    return factor_of


def noise(key, dims, deviation, most, cuts=(), kind=jnp.bfloat16):
    values = jax.random.normal(key, dims, jnp.float32) * deviation
    if len(cuts) > 0:
        values = block_scale(key, dims, cuts, -0.22, 0.18) * values
    return jnp.clip(values, min=-most, max=most).astype(kind)


def setup_inputs(seed: int = 0) -> dict:
    keys = jax.random.split(jax.random.key(seed), 6)
    return {
        "cons_old": noise(keys[0], (BLOCKS, NF, CELLS), 1.0, 6.0, ((0, 128),), jnp.float32),
        "flagged": draw_flagged(jax.random.fold_in(keys[5], 71), 0),
        "new_owner": draw_new_owner(jax.random.fold_in(keys[5], 71), 0),
        "diffusivity": jnp.clip(jnp.exp(jax.random.uniform(keys[3], (NF,), jnp.float32, math.log(0.02), math.log(0.1))), 0.02, 0.1),
        "courant": jnp.clip(jnp.exp(jax.random.uniform(keys[4], (NF,), jnp.float32, math.log(0.05), math.log(0.3))), 0.05, 0.3),
    }


def prolong_tables(extent):
    last = extent - 1
    rows = jnp.arange(extent, dtype=jnp.int32)
    lower = jnp.clip(rows - 1, 0, last)
    upper = jnp.clip(rows + 1, 0, last)
    width = (upper - lower).astype(jnp.float32)
    cols = jnp.arange(extent, dtype=jnp.int32)
    slopes = ((cols[None, :] == upper[:, None]).astype(jnp.float32) - (cols[None, :] == lower[:, None]).astype(jnp.float32)) / width[:, None]
    ident = (cols[None, :] == rows[:, None]).astype(jnp.float32)
    even = ident - 0.25 * slopes
    odd = ident + 0.25 * slopes
    refine_op = jnp.stack([even, odd], 1).reshape(2 * extent, extent)
    halves = refine_op.reshape(2, extent, extent)
    crossed = jnp.einsum('ybj,zck->jkyzbc', halves, halves, precision=lax.Precision.HIGHEST).reshape(extent * extent, 4 * extent * extent)
    return halves, crossed


def prolong(parents, halves, crossed):
    number, fields, volume = parents.shape
    extent = halves.shape[1]
    rows_flat = parents.reshape(number * fields * extent, extent * extent)
    planes = jnp.dot(rows_flat, crossed, precision=lax.Precision.HIGHEST, preferred_element_type=jnp.float32)
    planes = planes.reshape(number, fields, extent, 4, extent * extent)
    result = jnp.einsum('xai,nfiqc->nxqfac', halves, planes, precision=lax.Precision.HIGHEST)
    return result.reshape(number, 8, fields, volume)


def stencil_step(slab, diffusivity, courant):
    padded = jnp.pad(slab, ((0, 0), (1, 1), (0, 0), (0, 0)))
    behind = padded[:, :-2]
    forward = padded[:, 2:]
    beside_all = behind + forward + jnp.roll(slab, 1, 2) + jnp.roll(slab, -1, 2) + jnp.roll(slab, 1, 3) + jnp.roll(slab, -1, 3)
    diffuse = diffusivity[:, None, None, None]
    advect = courant[:, None, None, None]
    return slab + diffuse * (beside_all - 6.0 * slab) - advect * (slab - behind)


def reference(cons_old, flagged, new_owner, diffusivity, courant):
    slab = cons_old.reshape(BLOCKS, NF, EDGE, EDGE, EDGE).transpose(1, 0, 2, 3, 4).reshape(NF, BLOCKS * EDGE, EDGE, EDGE)
    stepped = stencil_step(slab, diffusivity, courant)
    coarse_next = stepped.reshape(NF, BLOCKS, EDGE, EDGE, EDGE).transpose(1, 0, 2, 3, 4).reshape(BLOCKS, NF, EDGE * EDGE * EDGE)
    slot_dev = jnp.arange(SLOTS, dtype=jnp.int32) // CAP
    slot_pos = jnp.arange(SLOTS, dtype=jnp.int32) % CAP
    before = jnp.sum((new_owner[None, :] < slot_dev[:, None]).astype(jnp.int32), axis=1)
    target = before + slot_pos
    clipped = jnp.minimum(target, PARENTS - 1)
    usable = (target < PARENTS) & (new_owner[clipped] == slot_dev)
    parents = jnp.where(usable[:, None, None], cons_old[flagged[clipped]], jnp.float32(0.0))
    halves, crossed = prolong_tables(EDGE)
    children = prolong(parents, halves, crossed)
    return coarse_next, children
```

```python
import functools

import jax
import jax.numpy as jnp
import numpy as np
from jax import lax
from jax.experimental import pallas as pl
from jax.experimental.pallas import tpu as pltpu
from jax.sharding import PartitionSpec as P

EDGE = 16
PLANE = EDGE * EDGE
CELLS = EDGE * PLANE
FIELDS = 8
AXES = ("morton", "lane")
CAP = 3
HOLD = 4
NEAR, FAR = 2, 1
STEP = 4


def refine_tables():
    ident = np.eye(EDGE)
    slope = np.zeros((EDGE, EDGE))
    for i in range(EDGE):
        low, high = max(i - 1, 0), min(i + 1, EDGE - 1)
        slope[i, high] += 1.0 / (high - low)
        slope[i, low] -= 1.0 / (high - low)
    fine = np.stack([ident - 0.25 * slope, ident + 0.25 * slope], 1).reshape(2, EDGE, EDGE)
    crossed = np.einsum("ybj,zck->jkyzbc", fine, fine).reshape(PLANE, 4 * PLANE)
    return crossed.astype(np.float32)


def beside_table():
    turn = np.roll(np.eye(EDGE), 1, 0) + np.roll(np.eye(EDGE), -1, 0)
    return (np.kron(turn, np.eye(EDGE)) + np.kron(np.eye(EDGE), turn)).astype(np.float32)


def swaps(count):
    even = [(i, i + 1) for i in range(0, count - 1, 2)]
    odd = [(i, i + 1) for i in range(1, count - 1, 2)]
    within = [(i, i + 2) for i in range(count - 2) if i % 4 < 2]
    across = [(i, i + 2) for i in range(count - 2) if i % 4 >= 2]
    return [pairs + [(b, a) for a, b in pairs] for pairs in (even, odd, within, across)]


def exchange(parts):
    count = lax.axis_size(AXES)
    return [lax.ppermute(part, AXES, pairs) for part, pairs in zip(parts, swaps(count))]


def channel(me, offset):
    near = jnp.where((me % 2 == 0) == (offset > 0), 0, 1)
    far = jnp.where((me % 4 < 2) == (offset > 0), 2, 3)
    return jnp.where(offset == 0, -1, jnp.where(jnp.abs(offset) == 1, near, far))


def first_from(ref, total, bound):
    low = jnp.int32(0)
    for power in reversed(range(total.bit_length())):
        probe = low + (1 << power)
        below = ref[jnp.minimum(probe, total) - 1] < bound
        low = jnp.where((probe <= total) & below, probe, low)
    return low


def pack_kernel(near, far, rims, rnd_ref, flagged_ref, owner_ref, cons_ref, *refs):
    outs, sem = refs[:4], refs[4]
    own = cons_ref.shape[0]
    total = flagged_ref.shape[0]
    me = lax.axis_index(AXES)
    started = []
    if rims:
        last = cons_ref.at[own - 1, :, pl.ds(CELLS - PLANE, PLANE)]
        first = cons_ref.at[0, :, pl.ds(0, PLANE)]
        for place, front, out in ((0, me % 2 == 0, outs[0]), (1, me % 2 == 1, outs[1])):
            target = out.at[:, pl.ds(near * CELLS, PLANE)]

            @pl.when(front)
            def _():
                pltpu.make_async_copy(last, target, sem.at[HOLD + place]).start()

            @pl.when(jnp.logical_not(front))
            def _():
                pltpu.make_async_copy(first, target, sem.at[HOLD + place]).start()

    start = first_from(flagged_ref, total, me * own)
    offsets = []
    for k in range(HOLD):
        place = jnp.minimum(start + k, total - 1)
        block = flagged_ref[place] - me * own
        mine = (start + k < total) & (block < own)
        block = jnp.clip(block, 0, own - 1)
        offset = owner_ref[place] - me
        offset = jnp.where(mine, offset, 0)
        rank = sum(((o == offset).astype(jnp.int32) for o in offsets), jnp.int32(0))
        offsets.append(jnp.where(mine, offset, 99))
        way = channel(me, offset)
        slot = rank - jnp.where(way < 2, rnd_ref[0], rnd_ref[1])
        fits = (way >= 0) & (slot >= 0) & (slot < jnp.where(way < 2, near, far))
        started.append(fits)
        for c, out in enumerate(outs):
            slots = near if c < 2 else far

            @pl.when(fits & (way == c))
            def _(c=c, out=out, slots=slots):
                column = pl.multiple_of(jnp.clip(slot, 0, slots - 1) * CELLS, CELLS)
                pltpu.make_async_copy(cons_ref.at[block], out.at[:, pl.ds(column, CELLS)], sem.at[k]).start()

    for k, fits in enumerate(started):

        @pl.when(fits)
        def _(k=k):
            pltpu.make_async_copy(cons_ref.at[0], outs[2].at[:, pl.ds(0, CELLS)], sem.at[k]).wait()

    if rims:
        for place in range(2):
            target = outs[place].at[:, pl.ds(near * CELLS, PLANE)]
            pltpu.make_async_copy(cons_ref.at[0, :, pl.ds(0, PLANE)], target, sem.at[HOLD + place]).wait()


def pack(rnd, flagged, owner, cons, near, far, rims):
    fields = cons.shape[1]
    wide = near * CELLS + (PLANE if rims else 0)
    shapes = [jax.ShapeDtypeStruct((fields, width), jnp.float32) for width in (wide, wide, far * CELLS, far * CELLS)]
    smem = pl.BlockSpec(memory_space=pltpu.SMEM)
    anywhere = pl.BlockSpec(memory_space=pl.ANY)
    return pl.pallas_call(
        functools.partial(pack_kernel, near, far, rims),
        out_shape=shapes,
        in_specs=[smem, smem, smem, anywhere],
        out_specs=[anywhere] * 4,
        scratch_shapes=[pltpu.SemaphoreType.DMA((HOLD + 2,))],
        cost_estimate=pl.CostEstimate(flops=0, bytes_accessed=1 << 20, transcendentals=0),
        name="pack",
    )(rnd, flagged, owner, cons)


def by_field(ref, fields):
    rows = lax.broadcasted_iota(jnp.int32, (fields, PLANE), 0)
    value = jnp.zeros((fields, PLANE), jnp.float32)
    for f in range(fields):
        value = jnp.where(rows == f, ref[f], value)
    return value


def split(value):
    high = value.astype(jnp.bfloat16)
    return high, (value - high.astype(jnp.float32)).astype(jnp.bfloat16)


def dot_split(value, table):
    return sum(jnp.dot(part, table, preferred_element_type=jnp.float32) for part in split(value))


def planes_of(block):
    return [block[:, x * PLANE : (x + 1) * PLANE] for x in range(EDGE)]


def coarse_kernel(diff_ref, cour_ref, block_ref, before_ref, after_ref, table_ref, out_ref, edge_ref):
    step = pl.program_id(0)
    steps = pl.num_programs(0)
    count, fields, _ = block_ref.shape
    diffuse = by_field(diff_ref, fields)
    courant = by_field(cour_ref, fields)
    centre = 1.0 - 6.0 * diffuse - courant
    back = diffuse + courant
    table = table_ref[...].astype(jnp.bfloat16)
    for b in range(count):
        planes = planes_of(block_ref[b])
        beside = dot_split(jnp.concatenate(planes, 0), table)
        if b > 0:
            low = block_ref[b - 1, :, pl.ds(CELLS - PLANE, PLANE)]
        else:
            low = jnp.where(step > 0, before_ref[0], 0.0)
        if b < count - 1:
            high = block_ref[b + 1, :, pl.ds(0, PLANE)]
        else:
            high = jnp.where(step < steps - 1, after_ref[0], 0.0)
        padded = [low] + planes + [high]
        for x in range(EDGE):
            ring = beside[x * fields : (x + 1) * fields]
            stepped = centre * padded[x + 1] + back * padded[x] + diffuse * (padded[x + 2] + ring)
            out_ref[b, :, pl.ds(x * PLANE, PLANE)] = stepped
            if b == 0 and x == 0:

                @pl.when(step == 0)
                def _():
                    edge_ref[0] = stepped

            if b == count - 1 and x == EDGE - 1:

                @pl.when(step == steps - 1)
                def _():
                    edge_ref[1] = stepped


def coarse(diffusivity, courant, cons):
    own, fields, cells = cons.shape
    smem = pl.BlockSpec(memory_space=pltpu.SMEM)
    return pl.pallas_call(
        coarse_kernel,
        grid=(own // STEP,),
        out_shape=[
            jax.ShapeDtypeStruct(cons.shape, jnp.float32),
            jax.ShapeDtypeStruct((2, fields, PLANE), jnp.float32),
        ],
        in_specs=[
            smem,
            smem,
            pl.BlockSpec((STEP, fields, cells), lambda i: (i, 0, 0)),
            pl.BlockSpec((1, fields, PLANE), lambda i: (jnp.maximum(i * STEP - 1, 0), 0, EDGE - 1)),
            pl.BlockSpec((1, fields, PLANE), lambda i: (jnp.minimum((i + 1) * STEP, own - 1), 0, 0)),
            pl.BlockSpec((PLANE, PLANE), lambda i: (0, 0)),
        ],
        out_specs=[
            pl.BlockSpec((STEP, fields, cells), lambda i: (i, 0, 0)),
            pl.BlockSpec((2, fields, PLANE), lambda i: (0, 0, 0)),
        ],
        compiler_params=pltpu.CompilerParams(vmem_limit_bytes=32 << 20),
        cost_estimate=pl.CostEstimate(flops=2 * 2 * own * EDGE * fields * PLANE * PLANE, bytes_accessed=8 << 20, transcendentals=0),
        name="coarse",
    )(diffusivity, courant, cons, cons, cons, jnp.asarray(beside_table()))


def refine(parent, table, out_ref):
    fields = parent.shape[0]
    fine = dot_split(jnp.concatenate(planes_of(parent), 0), table)
    rows = [fine[x * fields : (x + 1) * fields] for x in range(EDGE)]
    for x in range(EDGE):
        low, high = max(x - 1, 0), min(x + 1, EDGE - 1)
        slope = (rows[high] - rows[low]) * (0.25 / (high - low))
        half, place = divmod(2 * x, EDGE)
        for odd, value in enumerate((rows[x] - slope, rows[x] + slope)):
            for q in range(4):
                out_ref[half * 4 + q, :, pl.ds((place + odd) * PLANE, PLANE)] = value[:, q * PLANE : (q + 1) * PLANE]


def unpack_kernel(near, far, rims, *refs):
    if rims:
        rnd_ref, flagged_ref, owner_ref, diff_ref, cour_ref, cons_ref, *refs = refs
        parts, (edge_ref, table_ref, _, coarse_ref, children_ref), refs = refs[:4], refs[4:9], refs[9:]
        parent_ref, child_ref, rim_ref, sem = refs
    else:
        rnd_ref, flagged_ref, owner_ref, cons_ref, *refs = refs
        parts, (table_ref, _, children_ref), refs = refs[:4], refs[4:7], refs[7:]
        parent_ref, child_ref, sem = refs
    own = cons_ref.shape[0]
    total = flagged_ref.shape[0]
    me = lax.axis_index(AXES)
    start = first_from(owner_ref, total, me)
    offsets, loads, stores = [], [], []
    for s in range(CAP):
        place = jnp.minimum(start + s, total - 1)
        mine = (start + s < total) & (owner_ref[place] == me)
        block = flagged_ref[place]
        source = block // own
        offset = source - me
        rank = sum(((o == offset).astype(jnp.int32) for o in offsets), jnp.int32(0))
        offsets.append(jnp.where(mine, offset, 99))
        way = channel(me, offset)
        slot = rank - jnp.where(way < 2, rnd_ref[0], rnd_ref[1])
        fits = (slot >= 0) & (slot < jnp.where(way < 2, near, far))
        here = way < 0
        load = mine & (jnp.logical_not(here) & fits | here) if rims else mine & jnp.logical_not(here) & fits
        loads.append(load)
        stores.append(load | jnp.logical_not(mine) if rims else load)
        if rims:

            @pl.when(load & here)
            def _():
                local = jnp.clip(block - me * own, 0, own - 1)
                pltpu.make_async_copy(cons_ref.at[local], parent_ref.at[s], sem.at[s]).start()

        for c, part in enumerate(parts):
            slots = near if c < 2 else far

            @pl.when(load & (way == c))
            def _(c=c, part=part, slots=slots):
                column = pl.multiple_of(jnp.clip(slot, 0, slots - 1) * CELLS, CELLS)
                pltpu.make_async_copy(part.at[:, pl.ds(column, CELLS)], parent_ref.at[s], sem.at[s]).start()

    if rims:
        fields = cons_ref.shape[1]
        rim_at = pl.ds(near * CELLS, PLANE)
        fetch = [pltpu.make_async_copy(parts[c].at[:, rim_at], rim_ref.at[c], sem.at[2 * CAP + c]) for c in range(2)]
        for copy in fetch:
            copy.start()
        for copy in fetch:
            copy.wait()
        diffuse = by_field(diff_ref, fields)
        courant = by_field(cour_ref, fields)
        odd = me % 2 == 1
        low = jnp.where(odd, rim_ref[0], rim_ref[1])
        high = jnp.where(odd, rim_ref[1], rim_ref[0])
        rim_ref[2] = edge_ref[0] + (diffuse + courant) * low
        rim_ref[3] = edge_ref[1] + diffuse * high
        spots = (coarse_ref.at[0, :, pl.ds(0, PLANE)], coarse_ref.at[own - 1, :, pl.ds(CELLS - PLANE, PLANE)])
        ends = [pltpu.make_async_copy(rim_ref.at[2 + c], spots[c], sem.at[2 * CAP + 2 + c]) for c in range(2)]
        for copy in ends:
            copy.start()

    table = table_ref[...].astype(jnp.bfloat16)
    for s in range(CAP):

        @pl.when(loads[s])
        def _(s=s):
            pltpu.make_async_copy(cons_ref.at[0], parent_ref.at[s], sem.at[s]).wait()
            refine(parent_ref[s], table, child_ref.at[s])

        if rims:

            @pl.when(stores[s] & jnp.logical_not(loads[s]))
            def _(s=s):
                child_ref[s] = jnp.zeros(child_ref.shape[1:], jnp.float32)

        @pl.when(stores[s])
        def _(s=s):
            pltpu.make_async_copy(child_ref.at[s], children_ref.at[s], sem.at[CAP + s]).start()

    for s in range(CAP):

        @pl.when(stores[s])
        def _(s=s):
            pltpu.make_async_copy(child_ref.at[s], children_ref.at[s], sem.at[CAP + s]).wait()

    if rims:
        for copy in ends:
            copy.wait()


def unpack(rnd, flagged, owner, cons, parts, near, far, final=None, children=None):
    fields = cons.shape[1]
    smem = pl.BlockSpec(memory_space=pltpu.SMEM)
    vmem = pl.BlockSpec(memory_space=pltpu.VMEM)
    anywhere = pl.BlockSpec(memory_space=pl.ANY)
    hbm = pl.BlockSpec(memory_space=pltpu.HBM)
    family = jax.ShapeDtypeStruct((CAP, 8, fields, CELLS), jnp.float32)
    table = jnp.asarray(refine_tables())
    rims = final is not None
    scratch = [pltpu.VMEM((CAP, fields, CELLS), jnp.float32), pltpu.VMEM(family.shape, jnp.float32)]
    params = dict(
        compiler_params=pltpu.CompilerParams(vmem_limit_bytes=32 << 20),
        cost_estimate=pl.CostEstimate(flops=2 * 2 * CAP * EDGE * fields * PLANE * 4 * PLANE, bytes_accessed=5 << 20, transcendentals=0),
        name="unpack",
    )
    kernel = functools.partial(unpack_kernel, near, far, rims)
    if rims:
        diffusivity, courant, stepped, edges = final
        return pl.pallas_call(
            kernel,
            out_shape=[jax.ShapeDtypeStruct(stepped.shape, jnp.float32), family],
            in_specs=[smem] * 5 + [anywhere] * 5 + [vmem, vmem, hbm],
            out_specs=[hbm, hbm],
            scratch_shapes=scratch + [pltpu.VMEM((4, fields, PLANE), jnp.float32), pltpu.SemaphoreType.DMA((2 * CAP + 4,))],
            input_output_aliases={12: 0},
            **params,
        )(rnd, flagged, owner, diffusivity, courant, cons, *parts, edges, table, stepped)
    return pl.pallas_call(
        kernel,
        out_shape=family,
        in_specs=[smem] * 3 + [anywhere] * 5 + [vmem, hbm],
        out_specs=hbm,
        scratch_shapes=scratch + [pltpu.SemaphoreType.DMA((2 * CAP,))],
        input_output_aliases={9: 0},
        **params,
    )(rnd, flagged, owner, cons, *parts, table, children)


def rounds_left(flagged, owner, own):
    source = flagged // own
    offset = owner - source
    near, far = jnp.abs(offset) == 1, jnp.abs(offset) == 2
    key = source * 8 + offset
    left = jnp.int32(0)
    more = [jnp.any(kind[k:] & (key[k:] == key[:-k])) for kind, k in ((near, NEAR), (far, FAR), (far, FAR + 1))]
    near3, far2, far3 = (flag.astype(jnp.int32) for flag in more)
    return jnp.maximum(near3, far2 + far3)


def shards(cons_old, flagged, new_owner, diffusivity, courant):
    zero = jnp.zeros((2,), jnp.int32)
    parts = pack(zero, flagged, new_owner, cons_old, NEAR, FAR, True)
    arrived = exchange(parts)
    stepped, edges = coarse(diffusivity, courant, cons_old)
    final = (diffusivity, courant, stepped, edges)
    coarse_next, children = unpack(zero, flagged, new_owner, cons_old, arrived, NEAR, FAR, final)
    left = rounds_left(flagged, new_owner, cons_old.shape[0])

    def later(carry):
        turn, children = carry
        base = jnp.stack([NEAR + turn, FAR + turn]).astype(jnp.int32)
        parts = pack(base, flagged, new_owner, cons_old, 1, 1, False)
        children = unpack(base, flagged, new_owner, cons_old, exchange(parts), 1, 1, children=children)
        return turn + 1, children

    _, children = lax.while_loop(lambda carry: carry[0] < left, later, (jnp.int32(0), children))
    return coarse_next, children


def solution(mesh):
    in_specs = (P(AXES, None, None), P(), P(), P(), P())
    out_specs = (P(AXES, None, None), P(AXES, None, None, None))
    return jax.shard_map(shards, mesh=mesh, in_specs=in_specs, out_specs=out_specs, check_vma=False)
```

```python
import functools

import jax
import jax.numpy as jnp
from jax import lax
from jax.experimental import pallas as pl
from jax.experimental.pallas import tpu as pltpu
from jax.sharding import PartitionSpec as P

EDGE = 16
PLANE = EDGE * EDGE
CELLS = EDGE * PLANE
FIELDS = 8
AXES = ("morton", "lane")
CAP = 3
HOLD = 4
EVEN, ODD, WITHIN, ACROSS, HOME = range(5)
ROOM = (2, 1, 1, 1)
RIMS = (EVEN, ODD)
PLACES = [(way, rank) for way in range(HOME) for rank in range(ROOM[way])]
CHUNK = 8


def swaps(count):
    odd = [(i, i + 1) for i in range(1, count - 1, 2)]
    even = [(i, i + 1) for i in range(0, count - 1, 2)]
    across = [(i, i + 2) for i in range(count - 2) if i % 4 >= 2]
    within = [(i, i + 2) for i in range(count - 2) if i % 4 < 2]
    return [pairs + [(b, a) for a, b in pairs] for pairs in (even, odd, within, across)]


def exchange(parts):
    pairs = swaps(lax.axis_size(AXES))
    return [lax.ppermute(part, AXES, pairs[way]) for way, part in enumerate(parts)]


def channel(me, offset):
    near = jnp.where(((me & 1) == 1) == (offset > 0), ODD, EVEN)
    far = jnp.where(((me & 3) >= 2) == (offset > 0), ACROSS, WITHIN)
    return jnp.where(offset == 0, HOME, jnp.where(jnp.abs(offset) == 1, near, far))


def room(way):
    return sum((jnp.where(way == other, count, 0) for other, count in enumerate(ROOM)))


def holder(block, own):
    return block >> (own.bit_length() - 1) if own & (own - 1) == 0 else lax.div(block, jnp.int32(own))


def arrivals(flagged_ref, owner_ref, own, me):
    total = flagged_ref.shape[0]
    start = first_from(owner_ref, total, me)
    sources, found = [], []
    for s in range(CAP):
        place = jnp.minimum(start + s, total - 1)
        block = flagged_ref[place]
        mine = (start + s < total) & (owner_ref[place] == me)
        source = jnp.where(mine, holder(block, own), -1)
        rank = sum(((other == source).astype(jnp.int32) for other in sources), jnp.int32(0))
        sources.append(source)
        found.append((mine, block, channel(me, source - me), rank))
    return found


def first_from(ref, total, bound):
    low = jnp.int32(0)
    for power in reversed(range(total.bit_length())):
        probe = low + (1 << power)
        below = ref[jnp.minimum(probe, total) - 1] < bound
        low = jnp.where((probe <= total) & below, probe, low)
    return low


def rounds_left(flagged, owner, own):
    total = flagged.shape[1]
    rows = (8, total)
    source = jnp.broadcast_to(holder(flagged, own), rows)
    owner = jnp.broadcast_to(owner, rows)
    way = channel(source, owner - source)
    left = jnp.zeros(rows, jnp.int32)
    for rank in range(1, CAP):
        same = (pltpu.roll(source, total - rank, 1) == source) & (pltpu.roll(owner, total - rank, 1) == owner)
        left = jnp.maximum(left, jnp.where(same & (way < HOME), rank + 1 - room(way), 0))
    return jnp.max(left.astype(jnp.float32)).astype(jnp.int32)


def pack_kernel(later, *refs):
    if later:
        turn_ref, *refs = refs
    flagged_ref, owner_ref, cons_ref, *outs, sem = refs
    own = cons_ref.shape[0]
    total = flagged_ref.shape[0]
    me = lax.axis_index(AXES)
    rims = []
    if not later:
        last_plane = cons_ref.at[own - 1, :, pl.ds(CELLS - PLANE, PLANE)]
        first_plane = cons_ref.at[0, :, pl.ds(0, PLANE)]
        for c, way in enumerate(RIMS):
            target = outs[way].at[:, pl.ds(ROOM[way] * CELLS, PLANE)]
            rims.append(pltpu.make_async_copy(first_plane, target, sem.at[HOLD + c]))
            ahead = (me & 1) == c

            @pl.when(ahead)
            def _():
                pltpu.make_async_copy(last_plane, target, sem.at[HOLD + c]).start()

            @pl.when(jnp.logical_not(ahead))
            def _():
                pltpu.make_async_copy(first_plane, target, sem.at[HOLD + c]).start()

    start = first_from(flagged_ref, total, me * own)
    offsets, sent = [], []
    for k in range(HOLD):
        place = jnp.minimum(start + k, total - 1)
        block = flagged_ref[place] - me * own
        mine = (start + k < total) & (block < own)
        block = jnp.clip(block, 0, own - 1)
        offset = owner_ref[place] - me
        rank = sum(((other == offset).astype(jnp.int32) for other in offsets), jnp.int32(0))
        offsets.append(jnp.where(mine, offset, total))
        way = channel(me, offset)
        if later:
            fits = [(c, 0, mine & (way == c) & (rank == room(way) + turn_ref[0])) for c in range(HOME)]
        else:
            fits = [(c, r, mine & (way == c) & (rank == r)) for c, r in PLACES]
        for c, r, fit in fits:

            @pl.when(fit)
            def _():
                pltpu.make_async_copy(cons_ref.at[block], outs[c].at[:, pl.ds(r * CELLS, CELLS)], sem.at[k]).start()

        sent.append(functools.reduce(jnp.logical_or, [fit for _, _, fit in fits]))

    for k in range(HOLD):

        @pl.when(sent[k])
        def _():
            pltpu.make_async_copy(cons_ref.at[0], outs[0].at[:, pl.ds(0, CELLS)], sem.at[k]).wait()

    for copy in rims:
        copy.wait()


def pack(flagged, owner, cons, turn=None):
    fields = cons.shape[1]
    later = turn is not None
    widths = [CELLS] * HOME if later else [ROOM[way] * CELLS + (PLANE if way in RIMS else 0) for way in range(HOME)]
    smem = pl.BlockSpec(memory_space=pltpu.SMEM)
    anywhere = pl.BlockSpec(memory_space=pl.ANY)
    operands = ([turn] if later else []) + [flagged, owner, cons]
    return pl.pallas_call(
        functools.partial(pack_kernel, later),
        out_shape=[jax.ShapeDtypeStruct((fields, width), jnp.float32) for width in widths],
        in_specs=[smem] * (len(operands) - 1) + [anywhere],
        out_specs=[anywhere] * len(widths),
        scratch_shapes=[pltpu.SemaphoreType.DMA((HOLD + 2,))],
        compiler_params=pltpu.CompilerParams(vmem_limit_bytes=1 << 20),
        cost_estimate=pl.CostEstimate(flops=0, bytes_accessed=1 << 20, transcendentals=0),
        name="pack",
    )(*operands)


def by_field(ref, fields):
    rows = lax.broadcasted_iota(jnp.int32, (fields, PLANE), 0)
    value = jnp.zeros((fields, PLANE), jnp.float32)
    for f in range(fields):
        value = jnp.where(rows == f, ref[f], value)
    return value


def split(value):
    high = value.astype(jnp.bfloat16)
    return jnp.concatenate([high, (value - high.astype(jnp.float32)).astype(jnp.bfloat16)], 0)


def dot_split(parts, table):
    product = jnp.dot(parts, table, preferred_element_type=jnp.float32)
    half = parts.shape[0] // 2
    return product[:half] + product[half:]


def beside_table():
    rows = lax.broadcasted_iota(jnp.int32, (PLANE, PLANE), 0)
    columns = lax.broadcasted_iota(jnp.int32, (PLANE, PLANE), 1)
    apart = rows ^ columns
    along_y, along_z = (rows >> 4) - (columns >> 4) & 15, (rows & 15) - (columns & 15) & 15
    same_y, same_z = apart < EDGE, (apart & 15) == 0
    hit = same_z & ((along_y == 1) | (along_y == 15)) | same_y & ((along_z == 1) | (along_z == 15))
    return jnp.where(hit, 1.0, 0.0).astype(jnp.bfloat16)


def refine_values(fine, coarse):
    centre = fine >> 1
    low, high = jnp.maximum(centre - 1, 0), jnp.minimum(centre + 1, EDGE - 1)
    quarter = jnp.where(high - low == 1, 0.25, 0.125) * jnp.where((fine & 1) == 1, 1.0, -1.0)
    slope = jnp.where(coarse == high, quarter, 0.0) - jnp.where(coarse == low, quarter, 0.0)
    return slope + jnp.where(coarse == centre, 1.0, 0.0)


def fill_refine_table(table_ref):
    rows = lax.broadcasted_iota(jnp.int32, (PLANE, PLANE), 0)
    columns = lax.broadcasted_iota(jnp.int32, (PLANE, PLANE), 1)
    along_y = [refine_values(half * EDGE + (columns >> 4), rows >> 4) for half in range(2)]
    along_z = [refine_values(half * EDGE + (columns & 15), rows & 15) for half in range(2)]
    for q in range(4):
        table_ref[:, pl.ds(q * PLANE, PLANE)] = (along_y[q >> 1] * along_z[q & 1]).astype(jnp.bfloat16)


def coarse_kernel(flagged_ref, owner_ref, flagged_row, owner_row, diff_ref, cour_ref, cons_hbm, out_ref, edge_ref, table_ref, home_ref, plan_ref, left_ref, cons_ref, next_ref, sem):
    own, fields, _ = cons_ref.shape
    turns = own // CHUNK
    me = lax.axis_index(AXES)

    loads = 2 * turns
    part = own // loads

    def load(i):
        span = pl.ds(pl.multiple_of(i * part, part), part)
        return pltpu.make_async_copy(cons_hbm.at[span], cons_ref.at[span], sem.at[turns + i])

    for i in range(loads):
        load(i).start()
    fill_refine_table(table_ref)
    left_ref[0] = rounds_left(flagged_row[...], owner_row[...], own)
    diffuse = by_field(diff_ref, fields)
    courant = by_field(cour_ref, fields)
    centre = 1.0 - 6.0 * diffuse - courant
    back = diffuse + courant
    edge_ref[2] = diffuse
    edge_ref[3] = back

    beside = beside_table()

    def store(turn):
        span = pl.ds(pl.multiple_of(turn * CHUNK, CHUNK), CHUNK)
        return pltpu.make_async_copy(next_ref.at[span], out_ref.at[span], sem.at[turn])

    @pl.loop(0, turns)
    def _(turn):
        base = turn * CHUNK

        @pl.when(turn == 0)
        def _():
            load(0).wait()

        load(2 * turn + 1).wait()

        @pl.when(turn < turns - 1)
        def _():
            load(2 * turn + 2).wait()

        places = [(b, x) for b in range(CHUNK) for x in range(EDGE)]
        planes = [cons_ref[base + b, :, pl.ds(x * PLANE, PLANE)] for b, x in places]
        ring = dot_split(split(jnp.concatenate(planes, 0)), beside)
        low = cons_ref[jnp.maximum(base - 1, 0), :, pl.ds(CELLS - PLANE, PLANE)]
        high = cons_ref[jnp.minimum(base + CHUNK, own - 1), :, pl.ds(0, PLANE)]
        low = jnp.where(turn > 0, low, 0.0)
        high = jnp.where(turn < turns - 1, high, 0.0)
        padded = [low] + planes + [high]
        for i, (b, x) in enumerate(places):
            sides = padded[i + 2] + ring[i * fields : (i + 1) * fields]
            next_ref[base + b, :, pl.ds(x * PLANE, PLANE)] = centre * padded[i + 1] + back * padded[i] + diffuse * sides
        store(turn).start()

    for s, (mine, block, way, rank) in enumerate(arrivals(flagged_ref, owner_ref, own, me)):
        place = jnp.int32(len(PLACES))
        for i, (c, r) in enumerate(PLACES):
            place = jnp.where(mine & (way == c) & (rank == r), i, place)
        plan_ref[s] = place
        stays = mine & (way == HOME)

        @pl.when(stays)
        def _():
            home_ref[s] = cons_ref[jnp.clip(block - me * own, 0, own - 1)]

        @pl.when(jnp.logical_not(stays))
        def _():
            home_ref[s] = jnp.zeros(home_ref.shape[1:], jnp.float32)

    edge_ref[0] = next_ref[0, :, pl.ds(0, PLANE)]
    edge_ref[1] = next_ref[own - 1, :, pl.ds(CELLS - PLANE, PLANE)]
    for turn in range(turns):
        store(turn).wait()


def coarse(flagged, owner, diffusivity, courant, cons):
    own, fields, cells = cons.shape
    smem = pl.BlockSpec(memory_space=pltpu.SMEM)
    vmem = pl.BlockSpec(memory_space=pltpu.VMEM)
    hbm = pl.BlockSpec(memory_space=pltpu.HBM)
    return pl.pallas_call(
        coarse_kernel,
        out_shape=[
            pltpu.HBM(cons.shape, jnp.float32),
            jax.ShapeDtypeStruct((4, fields, PLANE), jnp.float32),
            jax.ShapeDtypeStruct((PLANE, 4 * PLANE), jnp.bfloat16),
            jax.ShapeDtypeStruct((CAP, fields, cells), jnp.float32),
            jax.ShapeDtypeStruct((CAP,), jnp.int32),
            jax.ShapeDtypeStruct((1,), jnp.int32),
        ],
        in_specs=[smem, smem, vmem, vmem, smem, smem, hbm],
        out_specs=[hbm, vmem, vmem, vmem, smem, smem],
        scratch_shapes=[
            pltpu.VMEM(cons.shape, jnp.float32),
            pltpu.VMEM(cons.shape, jnp.float32),
            pltpu.SemaphoreType.DMA((3 * (own // CHUNK),)),
        ],
        compiler_params=pltpu.CompilerParams(vmem_limit_bytes=20 << 20),
        cost_estimate=pl.CostEstimate(flops=2 * 2 * own * EDGE * fields * PLANE * PLANE, bytes_accessed=8 << 20, transcendentals=0),
        name="coarse",
    )(
        flagged,
        owner,
        flagged.reshape(1, -1),
        owner.reshape(1, -1),
        diffusivity,
        courant,
        pltpu.with_memory_space_constraint(cons, pltpu.HBM),
    )


def collect_kernel(own, turn_ref, flagged_ref, owner_ref, *refs):
    *parts, _, home_ref = refs
    me = lax.axis_index(AXES)
    for s, (mine, _, way, rank) in enumerate(arrivals(flagged_ref, owner_ref, own, me)):
        for c, part in enumerate(parts):

            @pl.when(mine & (way == c) & (rank == room(way) + turn_ref[0]))
            def _():
                home_ref[s] = part[...]


def collect(own, turn, flagged, owner, parts, home):
    smem = pl.BlockSpec(memory_space=pltpu.SMEM)
    vmem = pl.BlockSpec(memory_space=pltpu.VMEM)
    return pl.pallas_call(
        functools.partial(collect_kernel, own),
        out_shape=jax.ShapeDtypeStruct(home.shape, jnp.float32),
        in_specs=[smem] * 3 + [vmem] * (HOME + 1),
        out_specs=vmem,
        input_output_aliases={3 + HOME: 0},
        compiler_params=pltpu.CompilerParams(vmem_limit_bytes=8 << 20),
        name="collect",
    )(turn, flagged, owner, *parts, home)


def unpack_kernel(plan_ref, *refs):
    parts, (home_ref, edge_ref, table_ref, _, coarse_ref, children_ref, parent_ref, child_ref, rim_ref, sem) = refs[:HOME], refs[HOME:]
    own, fields, _ = coarse_ref.shape
    me = lax.axis_index(AXES)
    for s in range(CAP):
        spots = [parts[c].at[:, pl.ds(r * CELLS, CELLS)] for c, r in PLACES] + [home_ref.at[s]]
        for i, spot in enumerate(spots):

            @pl.when(plan_ref[s] == i)
            def _():
                parent_ref[s] = spot[...]

    rims = [parts[way][:, pl.ds(ROOM[way] * CELLS, PLANE)] for way in RIMS]
    odd = (me & 1) == 1
    rim_ref[0] = edge_ref[0] + edge_ref[3] * jnp.where(odd, rims[0], rims[1])
    rim_ref[1] = edge_ref[1] + edge_ref[2] * jnp.where(odd, rims[1], rims[0])
    spots = (coarse_ref.at[0, :, pl.ds(0, PLANE)], coarse_ref.at[own - 1, :, pl.ds(CELLS - PLANE, PLANE)])
    ends = [pltpu.make_async_copy(rim_ref.at[c], spots[c], sem.at[CAP * 8 + c]) for c in range(2)]
    for copy in ends:
        copy.start()

    def store(s, child):
        return pltpu.make_async_copy(child_ref.at[s, child], children_ref.at[s, child], sem.at[s * 8 + child])

    planes = [parent_ref[s, :, pl.ds(x * PLANE, PLANE)] for s in range(CAP) for x in range(EDGE)]
    parents = split(jnp.concatenate(planes, 0))
    for q in range(4):
        fine = dot_split(parents, table_ref[:, pl.ds(q * PLANE, PLANE)])
        for s in range(CAP):
            rows = [fine[(s * EDGE + x) * fields : (s * EDGE + x + 1) * fields] for x in range(EDGE)]
            for x in range(EDGE):
                low, high = max(x - 1, 0), min(x + 1, EDGE - 1)
                slope = (rows[high] - rows[low]) * (0.25 / (high - low))
                half, place = divmod(2 * x, EDGE)
                child_ref[s, half * 4 + q, :, pl.ds(place * PLANE, PLANE)] = rows[x] - slope
                child_ref[s, half * 4 + q, :, pl.ds((place + 1) * PLANE, PLANE)] = rows[x] + slope
            for half in range(2):
                store(s, half * 4 + q).start()

    for s in range(CAP):
        for child in range(8):
            store(s, child).wait()
    for copy in ends:
        copy.wait()


def unpack(plan, parts, home, edges, table, stepped):
    fields = stepped.shape[1]
    smem = pl.BlockSpec(memory_space=pltpu.SMEM)
    vmem = pl.BlockSpec(memory_space=pltpu.VMEM)
    hbm = pl.BlockSpec(memory_space=pltpu.HBM)
    family = pltpu.HBM((CAP, 8, fields, CELLS), jnp.float32)
    return pl.pallas_call(
        unpack_kernel,
        out_shape=[pltpu.HBM(stepped.shape, jnp.float32), family],
        in_specs=[smem] + [vmem] * (HOME + 3) + [hbm],
        out_specs=[hbm, hbm],
        scratch_shapes=[
            pltpu.VMEM((CAP, fields, CELLS), jnp.float32),
            pltpu.VMEM(family.shape, jnp.float32),
            pltpu.VMEM((2, fields, PLANE), jnp.float32),
            pltpu.SemaphoreType.DMA((CAP * 8 + 2,)),
        ],
        input_output_aliases={HOME + 4: 0},
        compiler_params=pltpu.CompilerParams(vmem_limit_bytes=24 << 20),
        cost_estimate=pl.CostEstimate(flops=2 * 2 * CAP * EDGE * fields * PLANE * 4 * PLANE, bytes_accessed=5 << 20, transcendentals=0),
        name="unpack",
    )(plan, *parts, home, edges, table, stepped)


def shards(cons_old, flagged, new_owner, diffusivity, courant):
    own = cons_old.shape[0]
    arrived = exchange(pack(flagged, new_owner, cons_old))
    stepped, edges, table, home, plan, left = coarse(flagged, new_owner, diffusivity, courant, cons_old)
    left = jnp.maximum(left.reshape(()), 0)

    def later(carry):
        turn, home = carry
        at = turn.reshape((1,))
        parts = exchange(pack(flagged, new_owner, cons_old, at))
        return turn + 1, collect(own, at, flagged, new_owner, parts, home)

    home, arrived = lax.optimization_barrier((home, arrived))
    _, home = lax.while_loop(lambda carry: carry[0] < left, later, (jnp.int32(0), home))
    return tuple(unpack(plan, arrived, home, edges, table, stepped))


def solution(mesh):
    in_specs = (P(AXES, None, None), P(), P(), P(), P())
    out_specs = (P(AXES, None, None), P(AXES, None, None, None))
    return jax.shard_map(shards, mesh=mesh, in_specs=in_specs, out_specs=out_specs, check_vma=False)
```

```python
import functools

import jax
import jax.numpy as jnp
from jax import lax
from jax.experimental import pallas as pl
from jax.experimental.pallas import tpu as pltpu
from jax.sharding import PartitionSpec as P

EDGE = 16
PLANE = EDGE * EDGE
CELLS = EDGE * PLANE
FIELDS = 8
AXES = ("morton", "lane")
CAP = 3
HOLD = 4
EVEN, ODD, WITHIN, ACROSS, HOME = range(5)
ROOM = (2, 1, 1, 1)
RIMS = (EVEN, ODD)
PLACES = [(way, rank) for way in range(HOME) for rank in range(ROOM[way])]
CHUNK = 8


def swaps(count):
    odd = [(i, i + 1) for i in range(1, count - 1, 2)]
    even = [(i, i + 1) for i in range(0, count - 1, 2)]
    across = [(i, i + 2) for i in range(count - 2) if i % 4 >= 2]
    within = [(i, i + 2) for i in range(count - 2) if i % 4 < 2]
    return [pairs + [(b, a) for a, b in pairs] for pairs in (even, odd, within, across)]


def exchange(parts):
    pairs = swaps(lax.axis_size(AXES))
    return [lax.ppermute(part, AXES, pairs[way]) for way, part in enumerate(parts)]


def channel(me, offset):
    near = jnp.where(((me & 1) == 1) == (offset > 0), ODD, EVEN)
    far = jnp.where(((me & 3) >= 2) == (offset > 0), ACROSS, WITHIN)
    return jnp.where(offset == 0, HOME, jnp.where(jnp.abs(offset) == 1, near, far))


def room(way):
    return sum((jnp.where(way == other, count, 0) for other, count in enumerate(ROOM)))


def holder(block, own):
    return block >> (own.bit_length() - 1) if own & (own - 1) == 0 else lax.div(block, jnp.int32(own))


def arrivals(flagged_ref, owner_ref, own, me):
    total = flagged_ref.shape[0]
    start = first_from(owner_ref, total, me)
    sources, found = [], []
    for s in range(CAP):
        place = jnp.minimum(start + s, total - 1)
        block = flagged_ref[place]
        mine = (start + s < total) & (owner_ref[place] == me)
        source = jnp.where(mine, holder(block, own), -1)
        rank = sum(((other == source).astype(jnp.int32) for other in sources), jnp.int32(0))
        sources.append(source)
        found.append((mine, block, channel(me, source - me), rank))
    return found


def first_from(ref, total, bound):
    low = jnp.int32(0)
    for power in reversed(range(total.bit_length())):
        probe = low + (1 << power)
        below = ref[jnp.minimum(probe, total) - 1] < bound
        low = jnp.where((probe <= total) & below, probe, low)
    return low


def rounds_left(flagged, owner, own):
    total = flagged.shape[1]
    rows = (8, total)
    source = jnp.broadcast_to(holder(flagged, own), rows)
    owner = jnp.broadcast_to(owner, rows)
    way = channel(source, owner - source)
    left = jnp.zeros(rows, jnp.int32)
    for rank in range(1, CAP):
        same = (pltpu.roll(source, total - rank, 1) == source) & (pltpu.roll(owner, total - rank, 1) == owner)
        left = jnp.maximum(left, jnp.where(same & (way < HOME), rank + 1 - room(way), 0))
    return jnp.max(left.astype(jnp.float32)).astype(jnp.int32)


def pack_kernel(later, *refs):
    if later:
        turn_ref, *refs = refs
    flagged_ref, owner_ref, cons_ref, *outs, sem = refs
    own = cons_ref.shape[0]
    total = flagged_ref.shape[0]
    me = lax.axis_index(AXES)
    rims = []
    if not later:
        last_plane = cons_ref.at[own - 1, :, pl.ds(CELLS - PLANE, PLANE)]
        first_plane = cons_ref.at[0, :, pl.ds(0, PLANE)]
        for c, way in enumerate(RIMS):
            target = outs[way].at[:, pl.ds(ROOM[way] * CELLS, PLANE)]
            rims.append(pltpu.make_async_copy(first_plane, target, sem.at[HOLD + c]))
            ahead = (me & 1) == c

            @pl.when(ahead)
            def _():
                pltpu.make_async_copy(last_plane, target, sem.at[HOLD + c]).start()

            @pl.when(jnp.logical_not(ahead))
            def _():
                pltpu.make_async_copy(first_plane, target, sem.at[HOLD + c]).start()

    start = first_from(flagged_ref, total, me * own)
    offsets, sent = [], []
    for k in range(HOLD):
        place = jnp.minimum(start + k, total - 1)
        block = flagged_ref[place] - me * own
        mine = (start + k < total) & (block < own)
        block = jnp.clip(block, 0, own - 1)
        offset = owner_ref[place] - me
        rank = sum(((other == offset).astype(jnp.int32) for other in offsets), jnp.int32(0))
        offsets.append(jnp.where(mine, offset, total))
        way = channel(me, offset)
        if later:
            fits = [(c, 0, mine & (way == c) & (rank == room(way) + turn_ref[0])) for c in range(HOME)]
        else:
            fits = [(c, r, mine & (way == c) & (rank == r)) for c, r in PLACES]
        for c, r, fit in fits:

            @pl.when(fit)
            def _():
                pltpu.make_async_copy(cons_ref.at[block], outs[c].at[:, pl.ds(r * CELLS, CELLS)], sem.at[k]).start()

        sent.append(functools.reduce(jnp.logical_or, [fit for _, _, fit in fits]))

    for k in range(HOLD):

        @pl.when(sent[k])
        def _():
            pltpu.make_async_copy(cons_ref.at[0], outs[0].at[:, pl.ds(0, CELLS)], sem.at[k]).wait()

    for copy in rims:
        copy.wait()


def pack(flagged, owner, cons, turn=None):
    fields = cons.shape[1]
    later = turn is not None
    widths = [CELLS] * HOME if later else [ROOM[way] * CELLS + (PLANE if way in RIMS else 0) for way in range(HOME)]
    smem = pl.BlockSpec(memory_space=pltpu.SMEM)
    anywhere = pl.BlockSpec(memory_space=pl.ANY)
    operands = ([turn] if later else []) + [flagged, owner, cons]
    return pl.pallas_call(
        functools.partial(pack_kernel, later),
        out_shape=[jax.ShapeDtypeStruct((fields, width), jnp.float32) for width in widths],
        in_specs=[smem] * (len(operands) - 1) + [anywhere],
        out_specs=[anywhere] * len(widths),
        scratch_shapes=[pltpu.SemaphoreType.DMA((HOLD + 2,))],
        compiler_params=pltpu.CompilerParams(vmem_limit_bytes=1 << 20),
        cost_estimate=pl.CostEstimate(flops=0, bytes_accessed=1 << 20, transcendentals=0),
        name="pack",
    )(*operands)


def by_field(ref, fields):
    rows = lax.broadcasted_iota(jnp.int32, (fields, PLANE), 0)
    value = jnp.zeros((fields, PLANE), jnp.float32)
    for f in range(fields):
        value = jnp.where(rows == f, ref[f], value)
    return value


def split(value):
    high = value.astype(jnp.bfloat16)
    return jnp.concatenate([high, (value - high.astype(jnp.float32)).astype(jnp.bfloat16)], 0)


def dot_split(parts, table):
    product = jnp.dot(parts, table, preferred_element_type=jnp.float32)
    half = parts.shape[0] // 2
    return product[:half] + product[half:]


def beside_table():
    rows = lax.broadcasted_iota(jnp.int32, (PLANE, PLANE), 0)
    columns = lax.broadcasted_iota(jnp.int32, (PLANE, PLANE), 1)
    apart = rows ^ columns
    along_y, along_z = (rows >> 4) - (columns >> 4) & 15, (rows & 15) - (columns & 15) & 15
    same_y, same_z = apart < EDGE, (apart & 15) == 0
    hit = same_z & ((along_y == 1) | (along_y == 15)) | same_y & ((along_z == 1) | (along_z == 15))
    return jnp.where(hit, 1.0, 0.0).astype(jnp.bfloat16)


def refine_values(fine, coarse):
    centre = fine >> 1
    low, high = jnp.maximum(centre - 1, 0), jnp.minimum(centre + 1, EDGE - 1)
    quarter = jnp.where(high - low == 1, 0.25, 0.125) * jnp.where((fine & 1) == 1, 1.0, -1.0)
    slope = jnp.where(coarse == high, quarter, 0.0) - jnp.where(coarse == low, quarter, 0.0)
    return slope + jnp.where(coarse == centre, 1.0, 0.0)


def refine_quarter(q):
    rows = lax.broadcasted_iota(jnp.int32, (PLANE, PLANE), 0)
    columns = lax.broadcasted_iota(jnp.int32, (PLANE, PLANE), 1)
    along_y = refine_values((q >> 1) * EDGE + (columns >> 4), rows >> 4)
    along_z = refine_values((q & 1) * EDGE + (columns & 15), rows & 15)
    return (along_y * along_z).astype(jnp.bfloat16)


def coarse_kernel(*refs):
    scalars, (flagged_hbm, owner_hbm, cons_hbm, out_ref, edge_ref, table_ref, home_ref, plan_ref, left_hbm), refs = refs[:4], refs[4:13], refs[13:]
    copies, (left_ref, flagged_row, owner_row, cons_ref, next_ref, sem, few) = refs[:4], refs[4:]
    flagged_ref, owner_ref, diff_ref, cour_ref = copies
    own, fields, _ = cons_ref.shape
    turns = own // CHUNK
    me = lax.axis_index(AXES)

    loads = 2 * turns
    part = own // loads

    def load(i):
        span = pl.ds(pl.multiple_of(i * part, part), part)
        return pltpu.make_async_copy(cons_hbm.at[span], cons_ref.at[span], sem.at[turns + i])

    few_copies = [pltpu.make_async_copy(*pair, few.at[i]) for i, pair in enumerate(zip((*scalars, flagged_hbm, owner_hbm), (*copies, flagged_row, owner_row)))]
    for copy in few_copies:
        copy.start()
    for i in range(loads):
        load(i).start()
    beside = beside_table()
    for copy in few_copies:
        copy.wait()
    left_ref[0] = rounds_left(flagged_row[...], owner_row[...], own)
    left_copy = pltpu.make_async_copy(left_ref, left_hbm, few.at[len(few_copies)])
    left_copy.start()
    diffuse = by_field(diff_ref, fields)
    courant = by_field(cour_ref, fields)
    centre = 1.0 - 6.0 * diffuse - courant
    back = diffuse + courant
    edge_ref[2] = diffuse
    edge_ref[3] = back

    def store(turn):
        span = pl.ds(pl.multiple_of(turn * CHUNK, CHUNK), CHUNK)
        return pltpu.make_async_copy(next_ref.at[span], out_ref.at[span], sem.at[turn])

    @pl.loop(0, turns)
    def _(turn):
        base = turn * CHUNK

        @pl.when(turn == 0)
        def _():
            load(0).wait()

        load(2 * turn + 1).wait()

        @pl.when(turn < turns - 1)
        def _():
            load(2 * turn + 2).wait()

        places = [(b, x) for b in range(CHUNK) for x in range(EDGE)]
        planes = [cons_ref[base + b, :, pl.ds(x * PLANE, PLANE)] for b, x in places]
        ring = dot_split(split(jnp.concatenate(planes, 0)), beside)
        low = cons_ref[jnp.maximum(base - 1, 0), :, pl.ds(CELLS - PLANE, PLANE)]
        high = cons_ref[jnp.minimum(base + CHUNK, own - 1), :, pl.ds(0, PLANE)]
        low = jnp.where(turn > 0, low, 0.0)
        high = jnp.where(turn < turns - 1, high, 0.0)
        padded = [low] + planes + [high]
        for i, (b, x) in enumerate(places):
            sides = padded[i + 2] + ring[i * fields : (i + 1) * fields]
            next_ref[base + b, :, pl.ds(x * PLANE, PLANE)] = centre * padded[i + 1] + back * padded[i] + diffuse * sides
        store(turn).start()

    for q in range(4):
        table_ref[:, pl.ds(q * PLANE, PLANE)] = refine_quarter(q)

    found = arrivals(flagged_ref, owner_ref, own, me)
    for s, (mine, _, way, rank) in enumerate(found):
        for i, (c, r) in enumerate(PLACES):
            comes = mine & (way == c) & (rank == r)
            plan_ref[s, i] = jnp.full(plan_ref.shape[2:], comes.astype(jnp.int32))

    for s, (mine, block, way, _) in enumerate(found):
        stays = mine & (way == HOME)

        @pl.when(stays)
        def _():
            home_ref[s] = cons_ref[jnp.clip(block - me * own, 0, own - 1)]

        @pl.when(jnp.logical_not(stays))
        def _():
            home_ref[s] = jnp.zeros(home_ref.shape[1:], jnp.float32)

    edge_ref[0] = next_ref[0, :, pl.ds(0, PLANE)]
    edge_ref[1] = next_ref[own - 1, :, pl.ds(CELLS - PLANE, PLANE)]
    for turn in range(turns):
        store(turn).wait()
    left_copy.wait()


def coarse(flagged, owner, diffusivity, courant, cons):
    own, fields, cells = cons.shape
    vmem = pl.BlockSpec(memory_space=pltpu.VMEM)
    hbm = pl.BlockSpec(memory_space=pltpu.HBM)
    return pl.pallas_call(
        coarse_kernel,
        out_shape=[
            pltpu.HBM(cons.shape, jnp.float32),
            jax.ShapeDtypeStruct((4, fields, PLANE), jnp.float32),
            jax.ShapeDtypeStruct((PLANE, 4 * PLANE), jnp.bfloat16),
            jax.ShapeDtypeStruct((CAP, fields, cells), jnp.float32),
            jax.ShapeDtypeStruct((CAP, len(PLACES), fields, 128), jnp.int32),
            pltpu.HBM((1,), jnp.int32),
        ],
        in_specs=[hbm] * 7,
        out_specs=[hbm, vmem, vmem, vmem, vmem, hbm],
        scratch_shapes=[
            *(pltpu.SMEM(value.shape, value.dtype) for value in (flagged, owner, diffusivity, courant)),
            pltpu.SMEM((1,), jnp.int32),
            pltpu.VMEM((1, flagged.shape[0]), jnp.int32),
            pltpu.VMEM((1, owner.shape[0]), jnp.int32),
            pltpu.VMEM(cons.shape, jnp.float32),
            pltpu.VMEM(cons.shape, jnp.float32),
            pltpu.SemaphoreType.DMA((3 * (own // CHUNK),)),
            pltpu.SemaphoreType.DMA((7,)),
        ],
        compiler_params=pltpu.CompilerParams(vmem_limit_bytes=20 << 20),
        cost_estimate=pl.CostEstimate(flops=2 * 2 * own * EDGE * fields * PLANE * PLANE, bytes_accessed=8 << 20, transcendentals=0),
        name="coarse",
    )(
        *(pltpu.with_memory_space_constraint(value, pltpu.HBM) for value in (flagged, owner, diffusivity, courant)),
        *(pltpu.with_memory_space_constraint(value.reshape(1, -1), pltpu.HBM) for value in (flagged, owner)),
        pltpu.with_memory_space_constraint(cons, pltpu.HBM),
    )


def collect_kernel(own, turn_ref, flagged_ref, owner_ref, *refs):
    *parts, _, home_ref = refs
    me = lax.axis_index(AXES)
    for s, (mine, _, way, rank) in enumerate(arrivals(flagged_ref, owner_ref, own, me)):
        for c, part in enumerate(parts):

            @pl.when(mine & (way == c) & (rank == room(way) + turn_ref[0]))
            def _():
                home_ref[s] = part[...]


def collect(own, turn, flagged, owner, parts, home):
    smem = pl.BlockSpec(memory_space=pltpu.SMEM)
    vmem = pl.BlockSpec(memory_space=pltpu.VMEM)
    return pl.pallas_call(
        functools.partial(collect_kernel, own),
        out_shape=jax.ShapeDtypeStruct(home.shape, jnp.float32),
        in_specs=[smem] * 3 + [vmem] * (HOME + 1),
        out_specs=vmem,
        input_output_aliases={3 + HOME: 0},
        compiler_params=pltpu.CompilerParams(vmem_limit_bytes=8 << 20),
        name="collect",
    )(turn, flagged, owner, *parts, home)


def unpack_kernel(plan_ref, *refs):
    parts, (home_ref, edge_ref, table_ref, _, coarse_ref, children_ref, child_ref, rim_ref, sem) = refs[:HOME], refs[HOME:]
    own, fields, _ = coarse_ref.shape
    me = lax.axis_index(AXES)
    rims = [parts[way][:, pl.ds(ROOM[way] * CELLS, PLANE)] for way in RIMS]
    odd = (me & 1) == 1
    rim_ref[0] = edge_ref[0] + edge_ref[3] * jnp.where(odd, rims[0], rims[1])
    rim_ref[1] = edge_ref[1] + edge_ref[2] * jnp.where(odd, rims[1], rims[0])
    spots = (coarse_ref.at[0, :, pl.ds(0, PLANE)], coarse_ref.at[own - 1, :, pl.ds(CELLS - PLANE, PLANE)])
    ends = [pltpu.make_async_copy(rim_ref.at[c], spots[c], sem.at[CAP * 8 + c]) for c in range(2)]
    for copy in ends:
        copy.start()

    def store(s, child):
        return pltpu.make_async_copy(child_ref.at[s, child], children_ref.at[s, child], sem.at[s * 8 + child])

    @pl.loop(0, CAP)
    def _(s):
        comes = [plan_ref[s, i] != 0 for i in range(len(PLACES))]
        planes = []
        for x in range(EDGE):
            halves = []
            for column in range(x * PLANE, (x + 1) * PLANE, 128):
                value = home_ref[s, :, pl.ds(column, 128)]
                for i, (c, r) in enumerate(PLACES):
                    value = jnp.where(comes[i], parts[c][:, pl.ds(r * CELLS + column, 128)], value)
                halves.append(value)
            planes.append(jnp.concatenate(halves, 1))
        parent = split(jnp.concatenate(planes, 0))
        for q in range(4):
            fine = dot_split(parent, table_ref[:, pl.ds(q * PLANE, PLANE)])
            rows = [fine[x * fields : (x + 1) * fields] for x in range(EDGE)]
            for x in range(EDGE):
                low, high = max(x - 1, 0), min(x + 1, EDGE - 1)
                slope = (rows[high] - rows[low]) * (0.25 / (high - low))
                half, place = divmod(2 * x, EDGE)
                child_ref[s, half * 4 + q, :, pl.ds(place * PLANE, PLANE)] = rows[x] - slope
                child_ref[s, half * 4 + q, :, pl.ds((place + 1) * PLANE, PLANE)] = rows[x] + slope
            for half in range(2):
                store(s, half * 4 + q).start()

    @pl.loop(0, CAP * 8)
    def _(i):
        store(i >> 3, i & 7).wait()

    for copy in ends:
        copy.wait()


def unpack(plan, parts, home, edges, table, stepped):
    fields = stepped.shape[1]
    vmem = pl.BlockSpec(memory_space=pltpu.VMEM)
    hbm = pl.BlockSpec(memory_space=pltpu.HBM)
    family = pltpu.HBM((CAP, 8, fields, CELLS), jnp.float32)
    return pl.pallas_call(
        unpack_kernel,
        out_shape=[pltpu.HBM(stepped.shape, jnp.float32), family],
        in_specs=[vmem] * (HOME + 4) + [hbm],
        out_specs=[hbm, hbm],
        scratch_shapes=[
            pltpu.VMEM(family.shape, jnp.float32),
            pltpu.VMEM((2, fields, PLANE), jnp.float32),
            pltpu.SemaphoreType.DMA((CAP * 8 + 2,)),
        ],
        input_output_aliases={HOME + 4: 0},
        compiler_params=pltpu.CompilerParams(vmem_limit_bytes=24 << 20),
        cost_estimate=pl.CostEstimate(flops=2 * 2 * CAP * EDGE * fields * PLANE * 4 * PLANE, bytes_accessed=5 << 20, transcendentals=0),
        name="unpack",
    )(plan, *parts, home, edges, table, stepped)


def shards(cons_old, flagged, new_owner, diffusivity, courant):
    own = cons_old.shape[0]
    arrived = exchange(pack(flagged, new_owner, cons_old))
    stepped, edges, table, home, plan, left = coarse(flagged, new_owner, diffusivity, courant, cons_old)
    left = jnp.maximum(left.reshape(()), 0)

    def later(carry):
        turn, home = carry
        at = turn.reshape((1,))
        parts = exchange(pack(flagged, new_owner, cons_old, at))
        return turn + 1, collect(own, at, flagged, new_owner, parts, home)

    home, arrived = lax.optimization_barrier((home, arrived))
    _, home = lax.while_loop(lambda carry: carry[0] < left, later, (jnp.int32(0), home))
    return tuple(unpack(plan, arrived, home, edges, table, stepped))


def solution(mesh):
    in_specs = (P(AXES, None, None), P(), P(), P(), P())
    out_specs = (P(AXES, None, None), P(AXES, None, None, None))
    return jax.shard_map(shards, mesh=mesh, in_specs=in_specs, out_specs=out_specs, check_vma=False)
```

```python
import functools

import jax
import jax.numpy as jnp
from jax import lax
from jax.experimental import pallas as pl
from jax.experimental.pallas import tpu as pltpu
from jax.sharding import PartitionSpec as P

EDGE = 16
PLANE = EDGE * EDGE
CELLS = EDGE * PLANE
FIELDS = 8
AXES = ("morton", "lane")
CAP = 3
HOLD = 4
ODD, EVEN, ACROSS, WITHIN, HOME = range(5)
ROOM = (2, 2, 1, 1)
RIMS = (EVEN, ODD)
PLACES = [(way, rank) for way in range(HOME) for rank in range(ROOM[way])]
CHUNK = 8


def swaps(count):
    odd = [(i, i + 1) for i in range(1, count - 1, 2)]
    even = [(i, i + 1) for i in range(0, count - 1, 2)]
    across = [(i, i + 2) for i in range(count - 2) if i % 4 >= 2]
    within = [(i, i + 2) for i in range(count - 2) if i % 4 < 2]
    return [pairs + [(b, a) for a, b in pairs] for pairs in (odd, even, across, within)]


def exchange(parts):
    pairs = swaps(lax.axis_size(AXES))
    return [lax.ppermute(part, AXES, pairs[way]) for way, part in enumerate(parts)]


def channel(me, offset):
    near = jnp.where(((me & 1) == 1) == (offset > 0), ODD, EVEN)
    far = jnp.where(((me & 3) >= 2) == (offset > 0), ACROSS, WITHIN)
    return jnp.where(offset == 0, HOME, jnp.where(jnp.abs(offset) == 1, near, far))


def room(way):
    return sum((jnp.where(way == other, count, 0) for other, count in enumerate(ROOM)))


def holder(block, own):
    return block >> (own.bit_length() - 1) if own & (own - 1) == 0 else lax.div(block, jnp.int32(own))


def arrivals(flagged_ref, owner_ref, own, me):
    total = flagged_ref.shape[0]
    start = first_from(owner_ref, total, me)
    sources, found = [], []
    for s in range(CAP):
        place = jnp.minimum(start + s, total - 1)
        block = flagged_ref[place]
        mine = (start + s < total) & (owner_ref[place] == me)
        source = jnp.where(mine, holder(block, own), -1)
        rank = sum(((other == source).astype(jnp.int32) for other in sources), jnp.int32(0))
        sources.append(source)
        found.append((mine, block, channel(me, source - me), rank))
    return found


def first_from(ref, total, bound):
    low = jnp.int32(0)
    for power in reversed(range(total.bit_length())):
        probe = low + (1 << power)
        below = ref[jnp.minimum(probe, total) - 1] < bound
        low = jnp.where((probe <= total) & below, probe, low)
    return low


def rounds_left(flagged, owner, own):
    total = flagged.shape[1]
    rows = (8, total)
    source = jnp.broadcast_to(holder(flagged, own), rows)
    owner = jnp.broadcast_to(owner, rows)
    way = channel(source, owner - source)
    left = jnp.zeros(rows, jnp.int32)
    for rank in range(1, CAP):
        same = (pltpu.roll(source, total - rank, 1) == source) & (pltpu.roll(owner, total - rank, 1) == owner)
        left = jnp.maximum(left, jnp.where(same & (way < HOME), rank + 1 - room(way), 0))
    return jnp.max(left.astype(jnp.float32)).astype(jnp.int32)


def pack_kernel(later, *refs):
    if later:
        turn_ref, *refs = refs
    flagged_ref, owner_ref, cons_ref, *outs, sem = refs
    own = cons_ref.shape[0]
    total = flagged_ref.shape[0]
    me = lax.axis_index(AXES)
    rims = []
    if not later:
        last_plane = cons_ref.at[own - 1, :, pl.ds(CELLS - PLANE, PLANE)]
        first_plane = cons_ref.at[0, :, pl.ds(0, PLANE)]
        for c, way in enumerate(RIMS):
            target = outs[way].at[:, pl.ds(ROOM[way] * CELLS, PLANE)]
            rims.append(pltpu.make_async_copy(first_plane, target, sem.at[HOLD + c]))
            ahead = (me & 1) == c

            @pl.when(ahead)
            def _():
                pltpu.make_async_copy(last_plane, target, sem.at[HOLD + c]).start()

            @pl.when(jnp.logical_not(ahead))
            def _():
                pltpu.make_async_copy(first_plane, target, sem.at[HOLD + c]).start()

    start = first_from(flagged_ref, total, me * own)
    offsets, sent = [], []
    for k in range(HOLD):
        place = jnp.minimum(start + k, total - 1)
        block = flagged_ref[place] - me * own
        mine = (start + k < total) & (block < own)
        block = jnp.clip(block, 0, own - 1)
        offset = owner_ref[place] - me
        rank = sum(((other == offset).astype(jnp.int32) for other in offsets), jnp.int32(0))
        offsets.append(jnp.where(mine, offset, total))
        way = channel(me, offset)
        if later:
            fits = [(c, 0, mine & (way == c) & (rank == room(way) + turn_ref[0])) for c in range(HOME)]
        else:
            fits = [(c, r, mine & (way == c) & (rank == r)) for c, r in PLACES]
        for c, r, fit in fits:

            @pl.when(fit)
            def _():
                pltpu.make_async_copy(cons_ref.at[block], outs[c].at[:, pl.ds(r * CELLS, CELLS)], sem.at[k]).start()

        sent.append(functools.reduce(jnp.logical_or, [fit for _, _, fit in fits]))

    for k in range(HOLD):

        @pl.when(sent[k])
        def _():
            pltpu.make_async_copy(cons_ref.at[0], outs[0].at[:, pl.ds(0, CELLS)], sem.at[k]).wait()

    for copy in rims:
        copy.wait()


def pack(flagged, owner, cons, turn=None):
    fields = cons.shape[1]
    later = turn is not None
    widths = [CELLS] * HOME if later else [ROOM[way] * CELLS + (PLANE if way in RIMS else 0) for way in range(HOME)]
    smem = pl.BlockSpec(memory_space=pltpu.SMEM)
    anywhere = pl.BlockSpec(memory_space=pl.ANY)
    operands = ([turn] if later else []) + [flagged, owner, cons]
    return pl.pallas_call(
        functools.partial(pack_kernel, later),
        out_shape=[jax.ShapeDtypeStruct((fields, width), jnp.float32) for width in widths],
        in_specs=[smem] * (len(operands) - 1) + [anywhere],
        out_specs=[anywhere] * len(widths),
        scratch_shapes=[pltpu.SemaphoreType.DMA((HOLD + 2,))],
        compiler_params=pltpu.CompilerParams(vmem_limit_bytes=1 << 20),
        cost_estimate=pl.CostEstimate(flops=0, bytes_accessed=1 << 20, transcendentals=0),
        name="pack",
    )(*operands)


def by_field(ref, fields):
    rows = lax.broadcasted_iota(jnp.int32, (fields, PLANE), 0)
    value = jnp.zeros((fields, PLANE), jnp.float32)
    for f in range(fields):
        value = jnp.where(rows == f, ref[f], value)
    return value


def split(value):
    high = value.astype(jnp.bfloat16)
    return jnp.concatenate([high, (value - high.astype(jnp.float32)).astype(jnp.bfloat16)], 0)


def dot_split(parts, table):
    product = jnp.dot(parts, table, preferred_element_type=jnp.float32)
    half = parts.shape[0] // 2
    return product[:half] + product[half:]


def beside_table():
    rows = lax.broadcasted_iota(jnp.int32, (PLANE, PLANE), 0)
    columns = lax.broadcasted_iota(jnp.int32, (PLANE, PLANE), 1)
    apart = rows ^ columns
    along_y, along_z = (rows >> 4) - (columns >> 4) & 15, (rows & 15) - (columns & 15) & 15
    same_y, same_z = apart < EDGE, (apart & 15) == 0
    hit = same_z & ((along_y == 1) | (along_y == 15)) | same_y & ((along_z == 1) | (along_z == 15))
    return jnp.where(hit, 1.0, 0.0).astype(jnp.bfloat16)


def refine_values(fine, coarse):
    centre = fine >> 1
    low, high = jnp.maximum(centre - 1, 0), jnp.minimum(centre + 1, EDGE - 1)
    quarter = jnp.where(high - low == 1, 0.25, 0.125) * jnp.where((fine & 1) == 1, 1.0, -1.0)
    slope = jnp.where(coarse == high, quarter, 0.0) - jnp.where(coarse == low, quarter, 0.0)
    return slope + jnp.where(coarse == centre, 1.0, 0.0)


def refine_quarter(q):
    rows = lax.broadcasted_iota(jnp.int32, (PLANE, PLANE), 0)
    columns = lax.broadcasted_iota(jnp.int32, (PLANE, PLANE), 1)
    along_y = refine_values((q >> 1) * EDGE + (columns >> 4), rows >> 4)
    along_z = refine_values((q & 1) * EDGE + (columns & 15), rows & 15)
    return (along_y * along_z).astype(jnp.bfloat16)


def coarse_kernel(*refs):
    scalars, (flagged_hbm, owner_hbm, cons_hbm, out_ref, edge_ref, table_ref, home_ref, plan_ref, left_hbm), refs = refs[:4], refs[4:13], refs[13:]
    copies, (left_ref, flagged_row, owner_row, cons_ref, next_ref, sem, few) = refs[:4], refs[4:]
    flagged_ref, owner_ref, diff_ref, cour_ref = copies
    own, fields, _ = cons_ref.shape
    turns = own // CHUNK
    me = lax.axis_index(AXES)

    loads = 2 * turns
    part = own // loads

    def load(i):
        span = pl.ds(pl.multiple_of(i * part, part), part)
        return pltpu.make_async_copy(cons_hbm.at[span], cons_ref.at[span], sem.at[turns + i])

    few_copies = [pltpu.make_async_copy(*pair, few.at[i]) for i, pair in enumerate(zip((*scalars, flagged_hbm, owner_hbm), (*copies, flagged_row, owner_row)))]
    for copy in few_copies:
        copy.start()
    for i in range(loads):
        load(i).start()
    beside = beside_table()
    for copy in few_copies:
        copy.wait()
    left_ref[0] = rounds_left(flagged_row[...], owner_row[...], own)
    left_copy = pltpu.make_async_copy(left_ref, left_hbm, few.at[len(few_copies)])
    left_copy.start()
    diffuse = by_field(diff_ref, fields)
    courant = by_field(cour_ref, fields)
    centre = 1.0 - 6.0 * diffuse - courant
    back = diffuse + courant
    edge_ref[2] = diffuse
    edge_ref[3] = back

    def store(turn):
        span = pl.ds(pl.multiple_of(turn * CHUNK, CHUNK), CHUNK)
        return pltpu.make_async_copy(next_ref.at[span], out_ref.at[span], sem.at[turn])

    @pl.loop(0, turns)
    def _(turn):
        base = turn * CHUNK

        @pl.when(turn == 0)
        def _():
            load(0).wait()

        load(2 * turn + 1).wait()

        @pl.when(turn < turns - 1)
        def _():
            load(2 * turn + 2).wait()

        places = [(b, x) for b in range(CHUNK) for x in range(EDGE)]
        planes = [cons_ref[base + b, :, pl.ds(x * PLANE, PLANE)] for b, x in places]
        ring = dot_split(split(jnp.concatenate(planes, 0)), beside)
        low = cons_ref[jnp.maximum(base - 1, 0), :, pl.ds(CELLS - PLANE, PLANE)]
        high = cons_ref[jnp.minimum(base + CHUNK, own - 1), :, pl.ds(0, PLANE)]
        low = jnp.where(turn > 0, low, 0.0)
        high = jnp.where(turn < turns - 1, high, 0.0)
        padded = [low] + planes + [high]
        for i, (b, x) in enumerate(places):
            sides = padded[i + 2] + ring[i * fields : (i + 1) * fields]
            next_ref[base + b, :, pl.ds(x * PLANE, PLANE)] = centre * padded[i + 1] + back * padded[i] + diffuse * sides
        store(turn).start()

    for q in range(4):
        table_ref[:, pl.ds(q * PLANE, PLANE)] = refine_quarter(q)

    found = arrivals(flagged_ref, owner_ref, own, me)
    for s, (mine, _, way, rank) in enumerate(found):
        for i, (c, r) in enumerate(PLACES):
            comes = mine & (way == c) & (rank == r)
            plan_ref[s, i] = jnp.full(plan_ref.shape[2:], comes.astype(jnp.int32))

    for s, (mine, block, way, _) in enumerate(found):
        stays = mine & (way == HOME)

        @pl.when(stays)
        def _():
            home_ref[s] = cons_ref[jnp.clip(block - me * own, 0, own - 1)]

        @pl.when(jnp.logical_not(stays))
        def _():
            home_ref[s] = jnp.zeros(home_ref.shape[1:], jnp.float32)

    edge_ref[0] = next_ref[0, :, pl.ds(0, PLANE)]
    edge_ref[1] = next_ref[own - 1, :, pl.ds(CELLS - PLANE, PLANE)]
    for turn in range(turns):
        store(turn).wait()
    left_copy.wait()


def coarse(flagged, owner, diffusivity, courant, cons):
    own, fields, cells = cons.shape
    vmem = pl.BlockSpec(memory_space=pltpu.VMEM)
    hbm = pl.BlockSpec(memory_space=pltpu.HBM)
    return pl.pallas_call(
        coarse_kernel,
        out_shape=[
            pltpu.HBM(cons.shape, jnp.float32),
            jax.ShapeDtypeStruct((4, fields, PLANE), jnp.float32),
            jax.ShapeDtypeStruct((PLANE, 4 * PLANE), jnp.bfloat16),
            jax.ShapeDtypeStruct((CAP, fields, cells), jnp.float32),
            jax.ShapeDtypeStruct((CAP, len(PLACES), fields, 128), jnp.int32),
            pltpu.HBM((1,), jnp.int32),
        ],
        in_specs=[hbm] * 7,
        out_specs=[hbm, vmem, vmem, vmem, vmem, hbm],
        scratch_shapes=[
            *(pltpu.SMEM(value.shape, value.dtype) for value in (flagged, owner, diffusivity, courant)),
            pltpu.SMEM((1,), jnp.int32),
            pltpu.VMEM((1, flagged.shape[0]), jnp.int32),
            pltpu.VMEM((1, owner.shape[0]), jnp.int32),
            pltpu.VMEM(cons.shape, jnp.float32),
            pltpu.VMEM(cons.shape, jnp.float32),
            pltpu.SemaphoreType.DMA((3 * (own // CHUNK),)),
            pltpu.SemaphoreType.DMA((7,)),
        ],
        compiler_params=pltpu.CompilerParams(vmem_limit_bytes=20 << 20),
        cost_estimate=pl.CostEstimate(flops=2 * 2 * own * EDGE * fields * PLANE * PLANE, bytes_accessed=8 << 20, transcendentals=0),
        name="coarse",
    )(
        *(pltpu.with_memory_space_constraint(value, pltpu.HBM) for value in (flagged, owner, diffusivity, courant)),
        *(pltpu.with_memory_space_constraint(value.reshape(1, -1), pltpu.HBM) for value in (flagged, owner)),
        pltpu.with_memory_space_constraint(cons, pltpu.HBM),
    )


def collect_kernel(own, turn_ref, flagged_ref, owner_ref, *refs):
    *parts, _, home_ref = refs
    me = lax.axis_index(AXES)
    for s, (mine, _, way, rank) in enumerate(arrivals(flagged_ref, owner_ref, own, me)):
        for c, part in enumerate(parts):

            @pl.when(mine & (way == c) & (rank == room(way) + turn_ref[0]))
            def _():
                home_ref[s] = part[...]


def collect(own, turn, flagged, owner, parts, home):
    smem = pl.BlockSpec(memory_space=pltpu.SMEM)
    vmem = pl.BlockSpec(memory_space=pltpu.VMEM)
    return pl.pallas_call(
        functools.partial(collect_kernel, own),
        out_shape=jax.ShapeDtypeStruct(home.shape, jnp.float32),
        in_specs=[smem] * 3 + [vmem] * (HOME + 1),
        out_specs=vmem,
        input_output_aliases={3 + HOME: 0},
        compiler_params=pltpu.CompilerParams(vmem_limit_bytes=8 << 20),
        name="collect",
    )(turn, flagged, owner, *parts, home)


def unpack_kernel(plan_ref, *refs):
    parts, (home_ref, edge_ref, table_ref, _, coarse_ref, children_ref, child_ref, rim_ref, sem) = refs[:HOME], refs[HOME:]
    own, fields, _ = coarse_ref.shape
    me = lax.axis_index(AXES)
    rims = [parts[way][:, pl.ds(ROOM[way] * CELLS, PLANE)] for way in RIMS]
    odd = (me & 1) == 1
    rim_ref[0] = edge_ref[0] + edge_ref[3] * jnp.where(odd, rims[0], rims[1])
    rim_ref[1] = edge_ref[1] + edge_ref[2] * jnp.where(odd, rims[1], rims[0])
    spots = (coarse_ref.at[0, :, pl.ds(0, PLANE)], coarse_ref.at[own - 1, :, pl.ds(CELLS - PLANE, PLANE)])
    ends = [pltpu.make_async_copy(rim_ref.at[c], spots[c], sem.at[CAP * 8 + c]) for c in range(2)]
    for copy in ends:
        copy.start()

    def store(s, child):
        return pltpu.make_async_copy(child_ref.at[s, child], children_ref.at[s, child], sem.at[s * 8 + child])

    @pl.loop(0, CAP)
    def _(s):
        comes = [plan_ref[s, i] != 0 for i in range(len(PLACES))]
        planes = []
        for x in range(EDGE):
            halves = []
            for column in range(x * PLANE, (x + 1) * PLANE, 128):
                value = home_ref[s, :, pl.ds(column, 128)]
                for i, (c, r) in enumerate(PLACES):
                    value = jnp.where(comes[i], parts[c][:, pl.ds(r * CELLS + column, 128)], value)
                halves.append(value)
            planes.append(jnp.concatenate(halves, 1))
        parent = split(jnp.concatenate(planes, 0))
        for q in range(4):
            fine = dot_split(parent, table_ref[:, pl.ds(q * PLANE, PLANE)])
            rows = [fine[x * fields : (x + 1) * fields] for x in range(EDGE)]
            for x in range(EDGE):
                low, high = max(x - 1, 0), min(x + 1, EDGE - 1)
                slope = (rows[high] - rows[low]) * (0.25 / (high - low))
                half, place = divmod(2 * x, EDGE)
                child_ref[s, half * 4 + q, :, pl.ds(place * PLANE, PLANE)] = rows[x] - slope
                child_ref[s, half * 4 + q, :, pl.ds((place + 1) * PLANE, PLANE)] = rows[x] + slope
            for half in range(2):
                store(s, half * 4 + q).start()

    @pl.loop(0, CAP * 8)
    def _(i):
        store(i >> 3, i & 7).wait()

    for copy in ends:
        copy.wait()


def unpack(plan, parts, home, edges, table, stepped):
    fields = stepped.shape[1]
    vmem = pl.BlockSpec(memory_space=pltpu.VMEM)
    hbm = pl.BlockSpec(memory_space=pltpu.HBM)
    family = pltpu.HBM((CAP, 8, fields, CELLS), jnp.float32)
    return pl.pallas_call(
        unpack_kernel,
        out_shape=[pltpu.HBM(stepped.shape, jnp.float32), family],
        in_specs=[vmem] * (HOME + 4) + [hbm],
        out_specs=[hbm, hbm],
        scratch_shapes=[
            pltpu.VMEM(family.shape, jnp.float32),
            pltpu.VMEM((2, fields, PLANE), jnp.float32),
            pltpu.SemaphoreType.DMA((CAP * 8 + 2,)),
        ],
        input_output_aliases={HOME + 4: 0},
        compiler_params=pltpu.CompilerParams(vmem_limit_bytes=24 << 20),
        cost_estimate=pl.CostEstimate(flops=2 * 2 * CAP * EDGE * fields * PLANE * 4 * PLANE, bytes_accessed=5 << 20, transcendentals=0),
        name="unpack",
    )(plan, *parts, home, edges, table, stepped)


def shards(cons_old, flagged, new_owner, diffusivity, courant):
    own = cons_old.shape[0]
    arrived = exchange(pack(flagged, new_owner, cons_old))
    stepped, edges, table, home, plan, left = coarse(flagged, new_owner, diffusivity, courant, cons_old)
    left = jnp.maximum(left.reshape(()), 0)

    def later(carry):
        turn, home = carry
        at = turn.reshape((1,))
        parts = exchange(pack(flagged, new_owner, cons_old, at))
        return turn + 1, collect(own, at, flagged, new_owner, parts, home)

    home, arrived = lax.optimization_barrier((home, arrived))
    _, home = lax.while_loop(lambda carry: carry[0] < left, later, (jnp.int32(0), home))
    return tuple(unpack(plan, arrived, home, edges, table, stepped))


def solution(mesh):
    in_specs = (P(AXES, None, None), P(), P(), P(), P())
    out_specs = (P(AXES, None, None), P(AXES, None, None, None))
    return jax.shard_map(shards, mesh=mesh, in_specs=in_specs, out_specs=out_specs, check_vma=False)
```

```python
import functools

import jax
import jax.numpy as jnp
from jax import lax
from jax.experimental import pallas as pl
from jax.experimental.pallas import tpu as pltpu
from jax.sharding import PartitionSpec as P

EDGE = 16
PLANE = EDGE * EDGE
CELLS = EDGE * PLANE
FIELDS = 8
AXES = ("morton", "lane")
CAP = 3
HOLD = 4
EVEN, ODD, WITHIN, ACROSS, HOME = range(5)
ROOM = (2, 1, 1, 1)
RIMS = (EVEN, ODD)
PLACES = [(way, rank) for way in range(HOME) for rank in range(ROOM[way])]
CHUNK = 8


def swaps(count):
    odd = [(i, i + 1) for i in range(1, count - 1, 2)]
    even = [(i, i + 1) for i in range(0, count - 1, 2)]
    across = [(i, i + 2) for i in range(count - 2) if i % 4 >= 2]
    within = [(i, i + 2) for i in range(count - 2) if i % 4 < 2]
    return [pairs + [(b, a) for a, b in pairs] for pairs in (even, odd, within, across)]


def exchange(parts):
    pairs = swaps(lax.axis_size(AXES))
    return [lax.ppermute(part, AXES, pairs[way]) for way, part in enumerate(parts)]


def channel(me, offset):
    near = jnp.where(((me & 1) == 1) == (offset > 0), ODD, EVEN)
    far = jnp.where(((me & 3) >= 2) == (offset > 0), ACROSS, WITHIN)
    return jnp.where(offset == 0, HOME, jnp.where(jnp.abs(offset) == 1, near, far))


def room(way):
    return sum((jnp.where(way == other, count, 0) for other, count in enumerate(ROOM)))


def holder(block, own):
    return block >> (own.bit_length() - 1) if own & (own - 1) == 0 else lax.div(block, jnp.int32(own))


def arrivals(flagged_ref, owner_ref, own, me):
    total = flagged_ref.shape[0]
    start = first_from(owner_ref, total, me)
    sources, found = [], []
    for s in range(CAP):
        place = jnp.minimum(start + s, total - 1)
        block = flagged_ref[place]
        mine = (start + s < total) & (owner_ref[place] == me)
        source = jnp.where(mine, holder(block, own), -1)
        rank = sum(((other == source).astype(jnp.int32) for other in sources), jnp.int32(0))
        sources.append(source)
        found.append((mine, block, channel(me, source - me), rank))
    return found


def first_from(ref, total, bound):
    low = jnp.int32(0)
    for power in reversed(range(total.bit_length())):
        probe = low + (1 << power)
        below = ref[jnp.minimum(probe, total) - 1] < bound
        low = jnp.where((probe <= total) & below, probe, low)
    return low


def rounds_left(flagged, owner, own):
    total = flagged.shape[1]
    rows = (8, total)
    source = jnp.broadcast_to(holder(flagged, own), rows)
    owner = jnp.broadcast_to(owner, rows)
    way = channel(source, owner - source)
    left = jnp.zeros(rows, jnp.int32)
    for rank in range(1, CAP):
        same = (pltpu.roll(source, total - rank, 1) == source) & (pltpu.roll(owner, total - rank, 1) == owner)
        left = jnp.maximum(left, jnp.where(same & (way < HOME), rank + 1 - room(way), 0))
    return jnp.max(left.astype(jnp.float32)).astype(jnp.int32)


def pack_kernel(later, *refs):
    if later:
        turn_ref, *refs = refs
    flagged_ref, owner_ref, cons_ref, *outs, sem = refs
    own = cons_ref.shape[0]
    total = flagged_ref.shape[0]
    me = lax.axis_index(AXES)
    rims = []
    if not later:
        last_plane = cons_ref.at[own - 1, :, pl.ds(CELLS - PLANE, PLANE)]
        first_plane = cons_ref.at[0, :, pl.ds(0, PLANE)]
        for c, way in enumerate(RIMS):
            target = outs[way].at[:, pl.ds(ROOM[way] * CELLS, PLANE)]
            rims.append(pltpu.make_async_copy(first_plane, target, sem.at[HOLD + c]))
            ahead = (me & 1) == c

            @pl.when(ahead)
            def _():
                pltpu.make_async_copy(last_plane, target, sem.at[HOLD + c]).start()

            @pl.when(jnp.logical_not(ahead))
            def _():
                pltpu.make_async_copy(first_plane, target, sem.at[HOLD + c]).start()

    start = first_from(flagged_ref, total, me * own)
    offsets, sent = [], []
    for k in range(HOLD):
        place = jnp.minimum(start + k, total - 1)
        block = flagged_ref[place] - me * own
        mine = (start + k < total) & (block < own)
        block = jnp.clip(block, 0, own - 1)
        offset = owner_ref[place] - me
        rank = sum(((other == offset).astype(jnp.int32) for other in offsets), jnp.int32(0))
        offsets.append(jnp.where(mine, offset, total))
        way = channel(me, offset)
        if later:
            fits = [(c, 0, mine & (way == c) & (rank == room(way) + turn_ref[0])) for c in range(HOME)]
        else:
            fits = [(c, r, mine & (way == c) & (rank == r)) for c, r in PLACES]
        for c, r, fit in fits:

            @pl.when(fit)
            def _():
                pltpu.make_async_copy(cons_ref.at[block], outs[c].at[:, pl.ds(r * CELLS, CELLS)], sem.at[k]).start()

        sent.append(functools.reduce(jnp.logical_or, [fit for _, _, fit in fits]))

    for k in range(HOLD):

        @pl.when(sent[k])
        def _():
            pltpu.make_async_copy(cons_ref.at[0], outs[0].at[:, pl.ds(0, CELLS)], sem.at[k]).wait()

    for copy in rims:
        copy.wait()


def pack(flagged, owner, cons, turn=None):
    fields = cons.shape[1]
    later = turn is not None
    widths = [CELLS] * HOME if later else [ROOM[way] * CELLS + (PLANE if way in RIMS else 0) for way in range(HOME)]
    smem = pl.BlockSpec(memory_space=pltpu.SMEM)
    anywhere = pl.BlockSpec(memory_space=pl.ANY)
    operands = ([turn] if later else []) + [flagged, owner, cons]
    return pl.pallas_call(
        functools.partial(pack_kernel, later),
        out_shape=[jax.ShapeDtypeStruct((fields, width), jnp.float32) for width in widths],
        in_specs=[smem] * (len(operands) - 1) + [anywhere],
        out_specs=[anywhere] * len(widths),
        scratch_shapes=[pltpu.SemaphoreType.DMA((HOLD + 2,))],
        compiler_params=pltpu.CompilerParams(vmem_limit_bytes=1 << 20),
        cost_estimate=pl.CostEstimate(flops=0, bytes_accessed=1 << 20, transcendentals=0),
        name="pack",
    )(*operands)


def by_field(ref, fields):
    rows = lax.broadcasted_iota(jnp.int32, (fields, PLANE), 0)
    value = jnp.zeros((fields, PLANE), jnp.float32)
    for f in range(fields):
        value = jnp.where(rows == f, ref[f], value)
    return value


def split(value):
    high = value.astype(jnp.bfloat16)
    return jnp.concatenate([high, (value - high.astype(jnp.float32)).astype(jnp.bfloat16)], 0)


def dot_split(parts, table):
    product = jnp.dot(parts, table, preferred_element_type=jnp.float32)
    half = parts.shape[0] // 2
    return product[:half] + product[half:]


def beside_table():
    rows = lax.broadcasted_iota(jnp.int32, (PLANE, PLANE), 0)
    columns = lax.broadcasted_iota(jnp.int32, (PLANE, PLANE), 1)
    apart = rows ^ columns
    along_y, along_z = (rows >> 4) - (columns >> 4) & 15, (rows & 15) - (columns & 15) & 15
    same_y, same_z = apart < EDGE, (apart & 15) == 0
    hit = same_z & ((along_y == 1) | (along_y == 15)) | same_y & ((along_z == 1) | (along_z == 15))
    return jnp.where(hit, 1.0, 0.0).astype(jnp.bfloat16)


def refine_values(fine, coarse):
    centre = fine >> 1
    low, high = jnp.maximum(centre - 1, 0), jnp.minimum(centre + 1, EDGE - 1)
    quarter = jnp.where(high - low == 1, 0.25, 0.125) * jnp.where((fine & 1) == 1, 1.0, -1.0)
    slope = jnp.where(coarse == high, quarter, 0.0) - jnp.where(coarse == low, quarter, 0.0)
    return slope + jnp.where(coarse == centre, 1.0, 0.0)


def refine_quarter(q):
    rows = lax.broadcasted_iota(jnp.int32, (PLANE, PLANE), 0)
    columns = lax.broadcasted_iota(jnp.int32, (PLANE, PLANE), 1)
    along_y = refine_values((q >> 1) * EDGE + (columns >> 4), rows >> 4)
    along_z = refine_values((q & 1) * EDGE + (columns & 15), rows & 15)
    return (along_y * along_z).astype(jnp.bfloat16)


def coarse_kernel(*refs):
    scalars, (flagged_hbm, owner_hbm, cons_hbm, out_ref, edge_ref, table_ref, home_ref, plan_ref, left_ref), refs = refs[:4], refs[4:13], refs[13:]
    copies, (flagged_row, owner_row, cons_ref, next_ref, sem, few) = refs[:4], refs[4:]
    flagged_ref, owner_ref, diff_ref, cour_ref = copies
    own, fields, _ = cons_ref.shape
    turns = own // CHUNK
    me = lax.axis_index(AXES)

    loads = 2 * turns
    part = own // loads

    def load(i):
        span = pl.ds(pl.multiple_of(i * part, part), part)
        return pltpu.make_async_copy(cons_hbm.at[span], cons_ref.at[span], sem.at[turns + i])

    few_copies = [pltpu.make_async_copy(*pair, few.at[i]) for i, pair in enumerate(zip((*scalars, flagged_hbm, owner_hbm), (*copies, flagged_row, owner_row)))]
    for copy in few_copies:
        copy.start()
    for i in range(loads):
        load(i).start()
    beside = beside_table()
    for copy in few_copies:
        copy.wait()
    left_ref[0] = rounds_left(flagged_row[...], owner_row[...], own)
    diffuse = by_field(diff_ref, fields)
    courant = by_field(cour_ref, fields)
    centre = 1.0 - 6.0 * diffuse - courant
    back = diffuse + courant
    edge_ref[2] = diffuse
    edge_ref[3] = back

    def store(turn):
        span = pl.ds(pl.multiple_of(turn * CHUNK, CHUNK), CHUNK)
        return pltpu.make_async_copy(next_ref.at[span], out_ref.at[span], sem.at[turn])

    @pl.loop(0, turns)
    def _(turn):
        base = turn * CHUNK

        @pl.when(turn == 0)
        def _():
            load(0).wait()

        load(2 * turn + 1).wait()

        @pl.when(turn < turns - 1)
        def _():
            load(2 * turn + 2).wait()

        places = [(b, x) for b in range(CHUNK) for x in range(EDGE)]
        planes = [cons_ref[base + b, :, pl.ds(x * PLANE, PLANE)] for b, x in places]
        ring = dot_split(split(jnp.concatenate(planes, 0)), beside)
        low = cons_ref[jnp.maximum(base - 1, 0), :, pl.ds(CELLS - PLANE, PLANE)]
        high = cons_ref[jnp.minimum(base + CHUNK, own - 1), :, pl.ds(0, PLANE)]
        low = jnp.where(turn > 0, low, 0.0)
        high = jnp.where(turn < turns - 1, high, 0.0)
        padded = [low] + planes + [high]
        for i, (b, x) in enumerate(places):
            sides = padded[i + 2] + ring[i * fields : (i + 1) * fields]
            next_ref[base + b, :, pl.ds(x * PLANE, PLANE)] = centre * padded[i + 1] + back * padded[i] + diffuse * sides
        store(turn).start()

    for q in range(4):
        table_ref[:, pl.ds(q * PLANE, PLANE)] = refine_quarter(q)

    found = arrivals(flagged_ref, owner_ref, own, me)
    for s, (mine, _, way, rank) in enumerate(found):
        for i, (c, r) in enumerate(PLACES):
            comes = mine & (way == c) & (rank == r)
            plan_ref[s, i] = jnp.full(plan_ref.shape[2:], comes.astype(jnp.int32))

    for s, (mine, block, way, _) in enumerate(found):
        stays = mine & (way == HOME)

        @pl.when(stays)
        def _():
            home_ref[s] = cons_ref[jnp.clip(block - me * own, 0, own - 1)]

        @pl.when(jnp.logical_not(stays))
        def _():
            home_ref[s] = jnp.zeros(home_ref.shape[1:], jnp.float32)

    edge_ref[0] = next_ref[0, :, pl.ds(0, PLANE)]
    edge_ref[1] = next_ref[own - 1, :, pl.ds(CELLS - PLANE, PLANE)]
    for turn in range(turns):
        store(turn).wait()


def coarse(flagged, owner, diffusivity, courant, cons):
    own, fields, cells = cons.shape
    vmem = pl.BlockSpec(memory_space=pltpu.VMEM)
    hbm = pl.BlockSpec(memory_space=pltpu.HBM)
    return pl.pallas_call(
        coarse_kernel,
        out_shape=[
            pltpu.HBM(cons.shape, jnp.float32),
            jax.ShapeDtypeStruct((4, fields, PLANE), jnp.float32),
            jax.ShapeDtypeStruct((PLANE, 4 * PLANE), jnp.bfloat16),
            jax.ShapeDtypeStruct((CAP, fields, cells), jnp.float32),
            jax.ShapeDtypeStruct((CAP, len(PLACES), fields, 128), jnp.int32),
            pltpu.SMEM((1,), jnp.int32),
        ],
        in_specs=[hbm] * 7,
        out_specs=[hbm, vmem, vmem, vmem, vmem, pl.BlockSpec(memory_space=pltpu.SMEM)],
        scratch_shapes=[
            *(pltpu.SMEM(value.shape, value.dtype) for value in (flagged, owner, diffusivity, courant)),
            pltpu.VMEM((1, flagged.shape[0]), jnp.int32),
            pltpu.VMEM((1, owner.shape[0]), jnp.int32),
            pltpu.VMEM(cons.shape, jnp.float32),
            pltpu.VMEM(cons.shape, jnp.float32),
            pltpu.SemaphoreType.DMA((3 * (own // CHUNK),)),
            pltpu.SemaphoreType.DMA((7,)),
        ],
        compiler_params=pltpu.CompilerParams(vmem_limit_bytes=20 << 20),
        cost_estimate=pl.CostEstimate(flops=2 * 2 * own * EDGE * fields * PLANE * PLANE, bytes_accessed=8 << 20, transcendentals=0),
        name="coarse",
    )(
        *(pltpu.with_memory_space_constraint(value, pltpu.HBM) for value in (flagged, owner, diffusivity, courant)),
        *(pltpu.with_memory_space_constraint(value.reshape(1, -1), pltpu.HBM) for value in (flagged, owner)),
        pltpu.with_memory_space_constraint(cons, pltpu.HBM),
    )


def collect_kernel(own, turn_ref, flagged_ref, owner_ref, *refs):
    *parts, _, home_ref = refs
    me = lax.axis_index(AXES)
    for s, (mine, _, way, rank) in enumerate(arrivals(flagged_ref, owner_ref, own, me)):
        for c, part in enumerate(parts):

            @pl.when(mine & (way == c) & (rank == room(way) + turn_ref[0]))
            def _():
                home_ref[s] = part[...]


def collect(own, turn, flagged, owner, parts, home):
    smem = pl.BlockSpec(memory_space=pltpu.SMEM)
    vmem = pl.BlockSpec(memory_space=pltpu.VMEM)
    return pl.pallas_call(
        functools.partial(collect_kernel, own),
        out_shape=jax.ShapeDtypeStruct(home.shape, jnp.float32),
        in_specs=[smem] * 3 + [vmem] * (HOME + 1),
        out_specs=vmem,
        input_output_aliases={3 + HOME: 0},
        compiler_params=pltpu.CompilerParams(vmem_limit_bytes=8 << 20),
        name="collect",
    )(turn, flagged, owner, *parts, home)


def unpack_kernel(plan_ref, *refs):
    parts, (home_ref, edge_ref, table_ref, _, coarse_ref, children_ref, child_ref, rim_ref, sem) = refs[:HOME], refs[HOME:]
    own, fields, _ = coarse_ref.shape
    me = lax.axis_index(AXES)
    rims = [parts[way][:, pl.ds(ROOM[way] * CELLS, PLANE)] for way in RIMS]
    odd = (me & 1) == 1
    rim_ref[0] = edge_ref[0] + edge_ref[3] * jnp.where(odd, rims[0], rims[1])
    rim_ref[1] = edge_ref[1] + edge_ref[2] * jnp.where(odd, rims[1], rims[0])
    spots = (coarse_ref.at[0, :, pl.ds(0, PLANE)], coarse_ref.at[own - 1, :, pl.ds(CELLS - PLANE, PLANE)])
    ends = [pltpu.make_async_copy(rim_ref.at[c], spots[c], sem.at[CAP * 8 + c]) for c in range(2)]
    for copy in ends:
        copy.start()

    def store(s, child):
        return pltpu.make_async_copy(child_ref.at[s, child], children_ref.at[s, child], sem.at[s * 8 + child])

    @pl.loop(0, CAP)
    def _(s):
        comes = [plan_ref[s, i] != 0 for i in range(len(PLACES))]
        planes = []
        for x in range(EDGE):
            halves = []
            for column in range(x * PLANE, (x + 1) * PLANE, 128):
                value = home_ref[s, :, pl.ds(column, 128)]
                for i, (c, r) in enumerate(PLACES):
                    value = jnp.where(comes[i], parts[c][:, pl.ds(r * CELLS + column, 128)], value)
                halves.append(value)
            planes.append(jnp.concatenate(halves, 1))
        parent = split(jnp.concatenate(planes, 0))
        for q in range(4):
            fine = dot_split(parent, table_ref[:, pl.ds(q * PLANE, PLANE)])
            rows = [fine[x * fields : (x + 1) * fields] for x in range(EDGE)]
            for x in range(EDGE):
                low, high = max(x - 1, 0), min(x + 1, EDGE - 1)
                slope = (rows[high] - rows[low]) * (0.25 / (high - low))
                half, place = divmod(2 * x, EDGE)
                child_ref[s, half * 4 + q, :, pl.ds(place * PLANE, PLANE)] = rows[x] - slope
                child_ref[s, half * 4 + q, :, pl.ds((place + 1) * PLANE, PLANE)] = rows[x] + slope
            for half in range(2):
                store(s, half * 4 + q).start()

    @pl.loop(0, CAP * 8)
    def _(i):
        store(i >> 3, i & 7).wait()

    for copy in ends:
        copy.wait()


def unpack(plan, parts, home, edges, table, stepped):
    fields = stepped.shape[1]
    vmem = pl.BlockSpec(memory_space=pltpu.VMEM)
    hbm = pl.BlockSpec(memory_space=pltpu.HBM)
    family = pltpu.HBM((CAP, 8, fields, CELLS), jnp.float32)
    return pl.pallas_call(
        unpack_kernel,
        out_shape=[pltpu.HBM(stepped.shape, jnp.float32), family],
        in_specs=[vmem] * (HOME + 4) + [hbm],
        out_specs=[hbm, hbm],
        scratch_shapes=[
            pltpu.VMEM(family.shape, jnp.float32),
            pltpu.VMEM((2, fields, PLANE), jnp.float32),
            pltpu.SemaphoreType.DMA((CAP * 8 + 2,)),
        ],
        input_output_aliases={HOME + 4: 0},
        compiler_params=pltpu.CompilerParams(vmem_limit_bytes=24 << 20),
        cost_estimate=pl.CostEstimate(flops=2 * 2 * CAP * EDGE * fields * PLANE * 4 * PLANE, bytes_accessed=5 << 20, transcendentals=0),
        name="unpack",
    )(plan, *parts, home, edges, table, stepped)


def shards(cons_old, flagged, new_owner, diffusivity, courant):
    own = cons_old.shape[0]
    arrived = exchange(pack(flagged, new_owner, cons_old))
    stepped, edges, table, home, plan, left = coarse(flagged, new_owner, diffusivity, courant, cons_old)
    left = left.reshape(())

    def later(carry):
        turn, home = carry
        at = turn.reshape((1,))
        parts = exchange(pack(flagged, new_owner, cons_old, at))
        return turn + 1, collect(own, at, flagged, new_owner, parts, home)

    home, arrived = lax.optimization_barrier((home, arrived))
    _, home = lax.while_loop(lambda carry: carry[0] < left, later, (jnp.int32(0), home))
    return tuple(unpack(plan, arrived, home, edges, table, stepped))


def solution(mesh):
    in_specs = (P(AXES, None, None), P(), P(), P(), P())
    out_specs = (P(AXES, None, None), P(AXES, None, None, None))
    return jax.shard_map(shards, mesh=mesh, in_specs=in_specs, out_specs=out_specs, check_vma=False)
```

```python
import functools

import jax
import jax.numpy as jnp
from jax import lax
from jax.experimental import pallas as pl
from jax.experimental.pallas import tpu as pltpu
from jax.sharding import PartitionSpec as P

EDGE = 16
PLANE = EDGE * EDGE
CELLS = EDGE * PLANE
FIELDS = 8
AXES = ("morton", "lane")
CAP = 3
HOLD = 4
EVEN, ODD, WITHIN, ACROSS, HOME = range(5)
ROOM = (2, 1, 1, 1)
RIMS = (EVEN, ODD)
PLACES = [(way, rank) for way in range(HOME) for rank in range(ROOM[way])]
KEPT, EMPTY = len(PLACES), len(PLACES) + 1
CHUNK = 8


def swaps(count):
    odd = [(i, i + 1) for i in range(1, count - 1, 2)]
    even = [(i, i + 1) for i in range(0, count - 1, 2)]
    across = [(i, i + 2) for i in range(count - 2) if i % 4 >= 2]
    within = [(i, i + 2) for i in range(count - 2) if i % 4 < 2]
    return [pairs + [(b, a) for a, b in pairs] for pairs in (even, odd, within, across)]


def exchange(parts):
    pairs = swaps(lax.axis_size(AXES))
    return [lax.ppermute(part, AXES, pairs[way]) for way, part in enumerate(parts)]


def channel(me, offset):
    near = jnp.where(((me & 1) == 1) == (offset > 0), ODD, EVEN)
    far = jnp.where(((me & 3) >= 2) == (offset > 0), ACROSS, WITHIN)
    return jnp.where(offset == 0, HOME, jnp.where(jnp.abs(offset) == 1, near, far))


def room(way):
    return sum((jnp.where(way == other, count, 0) for other, count in enumerate(ROOM)))


def holder(block, own):
    return block >> (own.bit_length() - 1) if own & (own - 1) == 0 else lax.div(block, jnp.int32(own))


def arrivals(flagged_ref, owner_ref, own, me):
    total = flagged_ref.shape[0]
    start = first_from(owner_ref, total, me)
    sources, found = [], []
    for s in range(CAP):
        place = jnp.minimum(start + s, total - 1)
        block = flagged_ref[place]
        mine = (start + s < total) & (owner_ref[place] == me)
        source = jnp.where(mine, holder(block, own), -1)
        rank = sum(((other == source).astype(jnp.int32) for other in sources), jnp.int32(0))
        sources.append(source)
        found.append((mine, block, channel(me, source - me), rank))
    return found


def first_from(ref, total, bound):
    low = jnp.int32(0)
    for power in reversed(range(total.bit_length())):
        probe = low + (1 << power)
        below = ref[jnp.minimum(probe, total) - 1] < bound
        low = jnp.where((probe <= total) & below, probe, low)
    return low


def rounds_left(flagged, owner, own):
    total = flagged.shape[1]
    rows = (8, total)
    source = jnp.broadcast_to(holder(flagged, own), rows)
    owner = jnp.broadcast_to(owner, rows)
    way = channel(source, owner - source)
    left = jnp.zeros(rows, jnp.int32)
    for rank in range(1, CAP):
        same = (pltpu.roll(source, total - rank, 1) == source) & (pltpu.roll(owner, total - rank, 1) == owner)
        left = jnp.maximum(left, jnp.where(same & (way < HOME), rank + 1 - room(way), 0))
    return jnp.max(left.astype(jnp.float32)).astype(jnp.int32)


def pack_kernel(later, *refs):
    if later:
        turn_ref, *refs = refs
    flagged_ref, owner_ref, cons_ref, *outs, sem = refs
    own = cons_ref.shape[0]
    total = flagged_ref.shape[0]
    me = lax.axis_index(AXES)
    rims = []
    if not later:
        last_plane = cons_ref.at[own - 1, :, pl.ds(CELLS - PLANE, PLANE)]
        first_plane = cons_ref.at[0, :, pl.ds(0, PLANE)]
        for c, way in enumerate(RIMS):
            target = outs[way].at[:, pl.ds(ROOM[way] * CELLS, PLANE)]
            rims.append(pltpu.make_async_copy(first_plane, target, sem.at[HOLD + c]))
            ahead = (me & 1) == c

            @pl.when(ahead)
            def _():
                pltpu.make_async_copy(last_plane, target, sem.at[HOLD + c]).start()

            @pl.when(jnp.logical_not(ahead))
            def _():
                pltpu.make_async_copy(first_plane, target, sem.at[HOLD + c]).start()

    start = first_from(flagged_ref, total, me * own)
    offsets, sent = [], []
    for k in range(HOLD):
        place = jnp.minimum(start + k, total - 1)
        block = flagged_ref[place] - me * own
        mine = (start + k < total) & (block < own)
        block = jnp.clip(block, 0, own - 1)
        offset = owner_ref[place] - me
        rank = sum(((other == offset).astype(jnp.int32) for other in offsets), jnp.int32(0))
        offsets.append(jnp.where(mine, offset, total))
        way = channel(me, offset)
        if later:
            fits = [(c, 0, mine & (way == c) & (rank == room(way) + turn_ref[0])) for c in range(HOME)]
        else:
            fits = [(c, r, mine & (way == c) & (rank == r)) for c, r in PLACES]
        for c, r, fit in fits:

            @pl.when(fit)
            def _():
                pltpu.make_async_copy(cons_ref.at[block], outs[c].at[:, pl.ds(r * CELLS, CELLS)], sem.at[k]).start()

        sent.append(functools.reduce(jnp.logical_or, [fit for _, _, fit in fits]))

    for k in range(HOLD):

        @pl.when(sent[k])
        def _():
            pltpu.make_async_copy(cons_ref.at[0], outs[0].at[:, pl.ds(0, CELLS)], sem.at[k]).wait()

    for copy in rims:
        copy.wait()


def pack(flagged, owner, cons, turn=None):
    fields = cons.shape[1]
    later = turn is not None
    widths = [CELLS] * HOME if later else [ROOM[way] * CELLS + (PLANE if way in RIMS else 0) for way in range(HOME)]
    smem = pl.BlockSpec(memory_space=pltpu.SMEM)
    anywhere = pl.BlockSpec(memory_space=pl.ANY)
    operands = ([turn] if later else []) + [flagged, owner, cons]
    return pl.pallas_call(
        functools.partial(pack_kernel, later),
        out_shape=[jax.ShapeDtypeStruct((fields, width), jnp.float32) for width in widths],
        in_specs=[smem] * (len(operands) - 1) + [anywhere],
        out_specs=[anywhere] * len(widths),
        scratch_shapes=[pltpu.SemaphoreType.DMA((HOLD + 2,))],
        compiler_params=pltpu.CompilerParams(vmem_limit_bytes=1 << 20),
        cost_estimate=pl.CostEstimate(flops=0, bytes_accessed=1 << 20, transcendentals=0),
        name="pack",
    )(*operands)


def by_field(ref, fields):
    rows = lax.broadcasted_iota(jnp.int32, (fields, PLANE), 0)
    value = jnp.zeros((fields, PLANE), jnp.float32)
    for f in range(fields):
        value = jnp.where(rows == f, ref[f], value)
    return value


def split(value):
    high = value.astype(jnp.bfloat16)
    return jnp.concatenate([high, (value - high.astype(jnp.float32)).astype(jnp.bfloat16)], 0)


def dot_split(parts, table):
    product = jnp.dot(parts, table, preferred_element_type=jnp.float32)
    half = parts.shape[0] // 2
    return product[:half] + product[half:]


def beside_table():
    rows = lax.broadcasted_iota(jnp.int32, (PLANE, PLANE), 0)
    columns = lax.broadcasted_iota(jnp.int32, (PLANE, PLANE), 1)
    apart = rows ^ columns
    along_y, along_z = (rows >> 4) - (columns >> 4) & 15, (rows & 15) - (columns & 15) & 15
    same_y, same_z = apart < EDGE, (apart & 15) == 0
    hit = same_z & ((along_y == 1) | (along_y == 15)) | same_y & ((along_z == 1) | (along_z == 15))
    return jnp.where(hit, 1.0, 0.0).astype(jnp.bfloat16)


def refine_values(fine, coarse):
    centre = fine >> 1
    low, high = jnp.maximum(centre - 1, 0), jnp.minimum(centre + 1, EDGE - 1)
    quarter = jnp.where(high - low == 1, 0.25, 0.125) * jnp.where((fine & 1) == 1, 1.0, -1.0)
    slope = jnp.where(coarse == high, quarter, 0.0) - jnp.where(coarse == low, quarter, 0.0)
    return slope + jnp.where(coarse == centre, 1.0, 0.0)


def refine_quarter(q):
    rows = lax.broadcasted_iota(jnp.int32, (PLANE, PLANE), 0)
    columns = lax.broadcasted_iota(jnp.int32, (PLANE, PLANE), 1)
    along_y = refine_values((q >> 1) * EDGE + (columns >> 4), rows >> 4)
    along_z = refine_values((q & 1) * EDGE + (columns & 15), rows & 15)
    return (along_y * along_z).astype(jnp.bfloat16)


def coarse_kernel(*refs):
    scalars, (flagged_hbm, owner_hbm, cons_hbm, out_ref, children_ref, edge_ref, table_ref, home_ref, plan_ref, left_ref), refs = refs[:4], refs[4:14], refs[14:]
    copies, (flagged_row, owner_row, cons_ref, next_ref, zero_ref, sem, few) = refs[:4], refs[4:]
    flagged_ref, owner_ref, diff_ref, cour_ref = copies
    own, fields, _ = cons_ref.shape
    turns = own // CHUNK
    me = lax.axis_index(AXES)

    loads = 2 * turns
    part = own // loads

    def load(i):
        span = pl.ds(pl.multiple_of(i * part, part), part)
        return pltpu.make_async_copy(cons_hbm.at[span], cons_ref.at[span], sem.at[turns + i])

    zero_ref[...] = jnp.zeros(zero_ref.shape, jnp.float32)

    def put(s):
        return pltpu.make_async_copy(zero_ref, children_ref.at[s], few.at[len(copies) + 2 + s])

    few_copies = [pltpu.make_async_copy(*pair, few.at[i]) for i, pair in enumerate(zip((*scalars, flagged_hbm, owner_hbm), (*copies, flagged_row, owner_row)))]
    for copy in few_copies:
        copy.start()
    for i in range(loads):
        load(i).start()
    beside = beside_table()
    for copy in few_copies:
        copy.wait()
    left_ref[0] = rounds_left(flagged_row[...], owner_row[...], own)
    found = arrivals(flagged_ref, owner_ref, own, me)
    for s, (mine, _, way, rank) in enumerate(found):
        place = jnp.where(mine, KEPT, EMPTY)
        for i, (c, r) in enumerate(PLACES):
            place = jnp.where(mine & (way == c) & (rank == r), i, place)
        plan_ref[s] = place
        pl.when(jnp.logical_not(mine))(put(s).start)

    diffuse = by_field(diff_ref, fields)
    courant = by_field(cour_ref, fields)
    centre = 1.0 - 6.0 * diffuse - courant
    back = diffuse + courant
    edge_ref[2] = diffuse
    edge_ref[3] = back

    def store(turn):
        span = pl.ds(pl.multiple_of(turn * CHUNK, CHUNK), CHUNK)
        return pltpu.make_async_copy(next_ref.at[span], out_ref.at[span], sem.at[turn])

    @pl.loop(0, turns)
    def _(turn):
        base = turn * CHUNK

        @pl.when(turn == 0)
        def _():
            load(0).wait()

        load(2 * turn + 1).wait()

        @pl.when(turn < turns - 1)
        def _():
            load(2 * turn + 2).wait()

        places = [(b, x) for b in range(CHUNK) for x in range(EDGE)]
        planes = [cons_ref[base + b, :, pl.ds(x * PLANE, PLANE)] for b, x in places]
        ring = dot_split(split(jnp.concatenate(planes, 0)), beside)
        low = cons_ref[jnp.maximum(base - 1, 0), :, pl.ds(CELLS - PLANE, PLANE)]
        high = cons_ref[jnp.minimum(base + CHUNK, own - 1), :, pl.ds(0, PLANE)]
        low = jnp.where(turn > 0, low, 0.0)
        high = jnp.where(turn < turns - 1, high, 0.0)
        padded = [low] + planes + [high]
        for i, (b, x) in enumerate(places):
            sides = padded[i + 2] + ring[i * fields : (i + 1) * fields]
            next_ref[base + b, :, pl.ds(x * PLANE, PLANE)] = centre * padded[i + 1] + back * padded[i] + diffuse * sides
        store(turn).start()

    for q in range(4):
        table_ref[:, pl.ds(q * PLANE, PLANE)] = refine_quarter(q)

    for s, (mine, block, way, _) in enumerate(found):
        stays = mine & (way == HOME)

        @pl.when(stays)
        def _():
            home_ref[s] = cons_ref[jnp.clip(block - me * own, 0, own - 1)]

        @pl.when(jnp.logical_not(stays))
        def _():
            home_ref[s] = jnp.zeros(home_ref.shape[1:], jnp.float32)

    edge_ref[0] = next_ref[0, :, pl.ds(0, PLANE)]
    edge_ref[1] = next_ref[own - 1, :, pl.ds(CELLS - PLANE, PLANE)]
    for turn in range(turns):
        store(turn).wait()
    for s, (mine, _, _, _) in enumerate(found):
        pl.when(jnp.logical_not(mine))(put(s).wait)


def coarse(flagged, owner, diffusivity, courant, cons):
    own, fields, cells = cons.shape
    smem = pl.BlockSpec(memory_space=pltpu.SMEM)
    vmem = pl.BlockSpec(memory_space=pltpu.VMEM)
    hbm = pl.BlockSpec(memory_space=pltpu.HBM)
    return pl.pallas_call(
        coarse_kernel,
        out_shape=[
            pltpu.HBM(cons.shape, jnp.float32),
            pltpu.HBM((CAP, 8, fields, cells), jnp.float32),
            jax.ShapeDtypeStruct((4, fields, PLANE), jnp.float32),
            jax.ShapeDtypeStruct((PLANE, 4 * PLANE), jnp.bfloat16),
            jax.ShapeDtypeStruct((CAP, fields, cells), jnp.float32),
            pltpu.SMEM((CAP,), jnp.int32),
            pltpu.SMEM((1,), jnp.int32),
        ],
        in_specs=[hbm] * 7,
        out_specs=[hbm, hbm, vmem, vmem, vmem, smem, smem],
        scratch_shapes=[
            *(pltpu.SMEM(value.shape, value.dtype) for value in (flagged, owner, diffusivity, courant)),
            pltpu.VMEM((1, flagged.shape[0]), jnp.int32),
            pltpu.VMEM((1, owner.shape[0]), jnp.int32),
            pltpu.VMEM(cons.shape, jnp.float32),
            pltpu.VMEM(cons.shape, jnp.float32),
            pltpu.VMEM((8, fields, cells), jnp.float32),
            pltpu.SemaphoreType.DMA((3 * (own // CHUNK),)),
            pltpu.SemaphoreType.DMA((6 + CAP,)),
        ],
        compiler_params=pltpu.CompilerParams(vmem_limit_bytes=20 << 20),
        cost_estimate=pl.CostEstimate(flops=2 * 2 * own * EDGE * fields * PLANE * PLANE, bytes_accessed=8 << 20, transcendentals=0),
        name="coarse",
    )(
        *(pltpu.with_memory_space_constraint(value, pltpu.HBM) for value in (flagged, owner, diffusivity, courant)),
        *(pltpu.with_memory_space_constraint(value.reshape(1, -1), pltpu.HBM) for value in (flagged, owner)),
        pltpu.with_memory_space_constraint(cons, pltpu.HBM),
    )


def collect_kernel(own, turn_ref, flagged_ref, owner_ref, *refs):
    *parts, _, home_ref = refs
    me = lax.axis_index(AXES)
    for s, (mine, _, way, rank) in enumerate(arrivals(flagged_ref, owner_ref, own, me)):
        for c, part in enumerate(parts):

            @pl.when(mine & (way == c) & (rank == room(way) + turn_ref[0]))
            def _():
                home_ref[s] = part[...]


def collect(own, turn, flagged, owner, parts, home):
    smem = pl.BlockSpec(memory_space=pltpu.SMEM)
    vmem = pl.BlockSpec(memory_space=pltpu.VMEM)
    return pl.pallas_call(
        functools.partial(collect_kernel, own),
        out_shape=jax.ShapeDtypeStruct(home.shape, jnp.float32),
        in_specs=[smem] * 3 + [vmem] * (HOME + 1),
        out_specs=vmem,
        input_output_aliases={3 + HOME: 0},
        compiler_params=pltpu.CompilerParams(vmem_limit_bytes=8 << 20),
        name="collect",
    )(turn, flagged, owner, *parts, home)


def unpack_kernel(plan_ref, *refs):
    parts, (home_ref, edge_ref, table_ref, _, _, coarse_ref, children_ref, parent_ref, child_ref, rim_ref, sem) = refs[:HOME], refs[HOME:]
    own, fields, _ = coarse_ref.shape
    me = lax.axis_index(AXES)
    rims = [parts[way][:, pl.ds(ROOM[way] * CELLS, PLANE)] for way in RIMS]
    odd = (me & 1) == 1
    rim_ref[0] = edge_ref[0] + edge_ref[3] * jnp.where(odd, rims[0], rims[1])
    rim_ref[1] = edge_ref[1] + edge_ref[2] * jnp.where(odd, rims[1], rims[0])
    spots = (coarse_ref.at[0, :, pl.ds(0, PLANE)], coarse_ref.at[own - 1, :, pl.ds(CELLS - PLANE, PLANE)])
    ends = [pltpu.make_async_copy(rim_ref.at[c], spots[c], sem.at[CAP + c]) for c in range(2)]
    for copy in ends:
        copy.start()

    def store(s, child):
        return pltpu.make_async_copy(child_ref.at[s, child], children_ref.at[s, child], sem.at[s])

    @pl.loop(0, CAP)
    def _(s):
        for i, (c, r) in enumerate([*PLACES, (None, None)]):

            @pl.when(plan_ref[s] == i)
            def _():
                parent_ref[...] = home_ref[s] if c is None else parts[c][:, pl.ds(r * CELLS, CELLS)]

        @pl.when(plan_ref[s] != EMPTY)
        def _():
            planes = [parent_ref[:, pl.ds(x * PLANE, PLANE)] for x in range(EDGE)]
            parent = split(jnp.concatenate(planes, 0))
            for q in range(4):
                fine = dot_split(parent, table_ref[:, pl.ds(q * PLANE, PLANE)])
                rows = [fine[x * fields : (x + 1) * fields] for x in range(EDGE)]
                for x in range(EDGE):
                    low, high = max(x - 1, 0), min(x + 1, EDGE - 1)
                    slope = (rows[high] - rows[low]) * (0.25 / (high - low))
                    half, place = divmod(2 * x, EDGE)
                    child_ref[s, half * 4 + q, :, pl.ds(place * PLANE, PLANE)] = rows[x] - slope
                    child_ref[s, half * 4 + q, :, pl.ds((place + 1) * PLANE, PLANE)] = rows[x] + slope
                for half in range(2):
                    store(s, half * 4 + q).start()

    for s in range(CAP):
        pl.when(plan_ref[s] != EMPTY)(pltpu.make_async_copy(child_ref.at[s], children_ref.at[s], sem.at[s]).wait)

    for copy in ends:
        copy.wait()


def unpack(plan, parts, home, edges, table, stepped, children):
    fields = stepped.shape[1]
    vmem = pl.BlockSpec(memory_space=pltpu.VMEM)
    hbm = pl.BlockSpec(memory_space=pltpu.HBM)
    family = pltpu.HBM((CAP, 8, fields, CELLS), jnp.float32)
    return pl.pallas_call(
        unpack_kernel,
        out_shape=[pltpu.HBM(stepped.shape, jnp.float32), family],
        in_specs=[pl.BlockSpec(memory_space=pltpu.SMEM)] + [vmem] * (HOME + 3) + [hbm, hbm],
        out_specs=[hbm, hbm],
        scratch_shapes=[
            pltpu.VMEM((fields, CELLS), jnp.float32),
            pltpu.VMEM(family.shape, jnp.float32),
            pltpu.VMEM((2, fields, PLANE), jnp.float32),
            pltpu.SemaphoreType.DMA((CAP + 2,)),
        ],
        input_output_aliases={HOME + 4: 0, HOME + 5: 1},
        compiler_params=pltpu.CompilerParams(vmem_limit_bytes=24 << 20),
        cost_estimate=pl.CostEstimate(flops=2 * 2 * CAP * EDGE * fields * PLANE * 4 * PLANE, bytes_accessed=5 << 20, transcendentals=0),
        name="unpack",
    )(plan, *parts, home, edges, table, stepped, children)


def shards(cons_old, flagged, new_owner, diffusivity, courant):
    own = cons_old.shape[0]
    arrived = exchange(pack(flagged, new_owner, cons_old))
    stepped, children, edges, table, home, plan, left = coarse(flagged, new_owner, diffusivity, courant, cons_old)
    left = left.reshape(())

    def later(carry):
        turn, home = carry
        at = turn.reshape((1,))
        parts = exchange(pack(flagged, new_owner, cons_old, at))
        return turn + 1, collect(own, at, flagged, new_owner, parts, home)

    home, arrived = lax.optimization_barrier((home, arrived))
    _, home = lax.while_loop(lambda carry: carry[0] < left, later, (jnp.int32(0), home))
    return tuple(unpack(plan, arrived, home, edges, table, stepped, children))


def solution(mesh):
    in_specs = (P(AXES, None, None), P(), P(), P(), P())
    out_specs = (P(AXES, None, None), P(AXES, None, None, None))
    return jax.shard_map(shards, mesh=mesh, in_specs=in_specs, out_specs=out_specs, check_vma=False)
```

```python
import functools

import jax
import jax.numpy as jnp
from jax import lax
from jax.experimental import pallas as pl
from jax.experimental.pallas import tpu as pltpu
from jax.sharding import PartitionSpec as P

EDGE = 16
PLANE = EDGE * EDGE
CELLS = EDGE * PLANE
FIELDS = 8
AXES = ("morton", "lane")
CAP = 3
HOLD = 4
EVEN, ODD, WITHIN, ACROSS, HOME = range(5)
ROOM = (2, 1, 1, 1)
RIMS = (EVEN, ODD)
PLACES = [(way, rank) for way in range(HOME) for rank in range(ROOM[way])]
KEPT, EMPTY = len(PLACES), len(PLACES) + 1
CHUNK = 8


def swaps(count):
    odd = [(i, i + 1) for i in range(1, count - 1, 2)]
    even = [(i, i + 1) for i in range(0, count - 1, 2)]
    across = [(i, i + 2) for i in range(count - 2) if i % 4 >= 2]
    within = [(i, i + 2) for i in range(count - 2) if i % 4 < 2]
    return [pairs + [(b, a) for a, b in pairs] for pairs in (even, odd, within, across)]


def exchange(parts):
    pairs = swaps(lax.axis_size(AXES))
    return [lax.ppermute(part, AXES, pairs[way]) for way, part in enumerate(parts)]


def channel(me, offset):
    near = jnp.where(((me & 1) == 1) == (offset > 0), ODD, EVEN)
    far = jnp.where(((me & 3) >= 2) == (offset > 0), ACROSS, WITHIN)
    return jnp.where(offset == 0, HOME, jnp.where(jnp.abs(offset) == 1, near, far))


def room(way):
    return sum((jnp.where(way == other, count, 0) for other, count in enumerate(ROOM)))


def holder(block, own):
    return block >> (own.bit_length() - 1) if own & (own - 1) == 0 else lax.div(block, jnp.int32(own))


def arrivals(flagged_ref, owner_ref, own, me):
    total = flagged_ref.shape[0]
    start = first_from(owner_ref, total, me)
    sources, found = [], []
    for s in range(CAP):
        place = jnp.minimum(start + s, total - 1)
        block = flagged_ref[place]
        mine = (start + s < total) & (owner_ref[place] == me)
        source = jnp.where(mine, holder(block, own), -1)
        rank = sum(((other == source).astype(jnp.int32) for other in sources), jnp.int32(0))
        sources.append(source)
        found.append((mine, block, channel(me, source - me), rank))
    return found


def first_from(ref, total, bound):
    low = jnp.int32(0)
    for power in reversed(range(total.bit_length())):
        probe = low + (1 << power)
        below = ref[jnp.minimum(probe, total) - 1] < bound
        low = jnp.where((probe <= total) & below, probe, low)
    return low


def rounds_left(flagged, owner, own):
    total = flagged.shape[1]
    rows = (8, total)
    source = jnp.broadcast_to(holder(flagged, own), rows)
    owner = jnp.broadcast_to(owner, rows)
    way = channel(source, owner - source)
    left = jnp.zeros(rows, jnp.int32)
    for rank in range(1, CAP):
        same = (pltpu.roll(source, total - rank, 1) == source) & (pltpu.roll(owner, total - rank, 1) == owner)
        left = jnp.maximum(left, jnp.where(same & (way < HOME), rank + 1 - room(way), 0))
    return jnp.max(left.astype(jnp.float32)).astype(jnp.int32)


def pack_kernel(later, *refs):
    if later:
        turn_ref, *refs = refs
    flagged_ref, owner_ref, cons_ref, *outs, sem = refs
    own = cons_ref.shape[0]
    total = flagged_ref.shape[0]
    me = lax.axis_index(AXES)
    rims = []
    if not later:
        last_plane = cons_ref.at[own - 1, :, pl.ds(CELLS - PLANE, PLANE)]
        first_plane = cons_ref.at[0, :, pl.ds(0, PLANE)]
        for c, way in enumerate(RIMS):
            target = outs[way].at[:, pl.ds(ROOM[way] * CELLS, PLANE)]
            rims.append(pltpu.make_async_copy(first_plane, target, sem.at[HOLD + c]))
            ahead = (me & 1) == c

            @pl.when(ahead)
            def _():
                pltpu.make_async_copy(last_plane, target, sem.at[HOLD + c]).start()

            @pl.when(jnp.logical_not(ahead))
            def _():
                pltpu.make_async_copy(first_plane, target, sem.at[HOLD + c]).start()

    start = first_from(flagged_ref, total, me * own)
    offsets, sent = [], []
    for k in range(HOLD):
        place = jnp.minimum(start + k, total - 1)
        block = flagged_ref[place] - me * own
        mine = (start + k < total) & (block < own)
        block = jnp.clip(block, 0, own - 1)
        offset = owner_ref[place] - me
        rank = sum(((other == offset).astype(jnp.int32) for other in offsets), jnp.int32(0))
        offsets.append(jnp.where(mine, offset, total))
        way = channel(me, offset)
        if later:
            fits = [(c, 0, mine & (way == c) & (rank == room(way) + turn_ref[0])) for c in range(HOME)]
        else:
            fits = [(c, r, mine & (way == c) & (rank == r)) for c, r in PLACES]
        for c, r, fit in fits:

            @pl.when(fit)
            def _():
                pltpu.make_async_copy(cons_ref.at[block], outs[c].at[:, pl.ds(r * CELLS, CELLS)], sem.at[k]).start()

        sent.append(functools.reduce(jnp.logical_or, [fit for _, _, fit in fits]))

    for k in range(HOLD):

        @pl.when(sent[k])
        def _():
            pltpu.make_async_copy(cons_ref.at[0], outs[0].at[:, pl.ds(0, CELLS)], sem.at[k]).wait()

    for copy in rims:
        copy.wait()


def pack(flagged, owner, cons, turn=None):
    fields = cons.shape[1]
    later = turn is not None
    widths = [CELLS] * HOME if later else [ROOM[way] * CELLS + (PLANE if way in RIMS else 0) for way in range(HOME)]
    smem = pl.BlockSpec(memory_space=pltpu.SMEM)
    anywhere = pl.BlockSpec(memory_space=pl.ANY)
    operands = ([turn] if later else []) + [flagged, owner, cons]
    return pl.pallas_call(
        functools.partial(pack_kernel, later),
        out_shape=[jax.ShapeDtypeStruct((fields, width), jnp.float32) for width in widths],
        in_specs=[smem] * (len(operands) - 1) + [anywhere],
        out_specs=[anywhere] * len(widths),
        scratch_shapes=[pltpu.SemaphoreType.DMA((HOLD + 2,))],
        compiler_params=pltpu.CompilerParams(vmem_limit_bytes=1 << 20),
        cost_estimate=pl.CostEstimate(flops=0, bytes_accessed=1 << 20, transcendentals=0),
        name="pack",
    )(*operands)


def by_field(ref, fields):
    rows = lax.broadcasted_iota(jnp.int32, (fields, PLANE), 0)
    value = jnp.zeros((fields, PLANE), jnp.float32)
    for f in range(fields):
        value = jnp.where(rows == f, ref[f], value)
    return value


def split(value):
    high = value.astype(jnp.bfloat16)
    return jnp.concatenate([high, (value - high.astype(jnp.float32)).astype(jnp.bfloat16)], 0)


def dot_split(parts, table):
    product = jnp.dot(parts, table, preferred_element_type=jnp.float32)
    half = parts.shape[0] // 2
    return product[:half] + product[half:]


def beside_table():
    rows = lax.broadcasted_iota(jnp.int32, (PLANE, PLANE), 0)
    columns = lax.broadcasted_iota(jnp.int32, (PLANE, PLANE), 1)
    apart = rows ^ columns
    along_y, along_z = (rows >> 4) - (columns >> 4) & 15, (rows & 15) - (columns & 15) & 15
    same_y, same_z = apart < EDGE, (apart & 15) == 0
    hit = same_z & ((along_y == 1) | (along_y == 15)) | same_y & ((along_z == 1) | (along_z == 15))
    return jnp.where(hit, 1.0, 0.0).astype(jnp.bfloat16)


def refine_values(fine, coarse):
    centre = fine >> 1
    low, high = jnp.maximum(centre - 1, 0), jnp.minimum(centre + 1, EDGE - 1)
    quarter = jnp.where(high - low == 1, 0.25, 0.125) * jnp.where((fine & 1) == 1, 1.0, -1.0)
    slope = jnp.where(coarse == high, quarter, 0.0) - jnp.where(coarse == low, quarter, 0.0)
    return slope + jnp.where(coarse == centre, 1.0, 0.0)


def refine_quarter(q):
    rows = lax.broadcasted_iota(jnp.int32, (PLANE, PLANE), 0)
    columns = lax.broadcasted_iota(jnp.int32, (PLANE, PLANE), 1)
    along_y = refine_values((q >> 1) * EDGE + (columns >> 4), rows >> 4)
    along_z = refine_values((q & 1) * EDGE + (columns & 15), rows & 15)
    return (along_y * along_z).astype(jnp.bfloat16)


def coarse_kernel(*refs):
    scalars, (flagged_hbm, owner_hbm, cons_hbm, out_ref, children_ref, edge_ref, table_ref, home_ref, plan_ref, left_ref), refs = refs[:4], refs[4:14], refs[14:]
    copies, (flagged_row, owner_row, cons_ref, next_ref, zero_ref, sem, few) = refs[:4], refs[4:]
    flagged_ref, owner_ref, diff_ref, cour_ref = copies
    own, fields, _ = cons_ref.shape
    turns = own // CHUNK
    me = lax.axis_index(AXES)

    loads = 2 * turns
    part = own // loads

    def load(i):
        span = pl.ds(pl.multiple_of(i * part, part), part)
        return pltpu.make_async_copy(cons_hbm.at[span], cons_ref.at[span], sem.at[turns + i])

    zero_ref[...] = jnp.zeros(zero_ref.shape, jnp.float32)

    def put(s):
        return pltpu.make_async_copy(zero_ref, children_ref.at[s], few.at[len(copies) + 2 + s])

    few_copies = [pltpu.make_async_copy(*pair, few.at[i]) for i, pair in enumerate(zip((*scalars, flagged_hbm, owner_hbm), (*copies, flagged_row, owner_row)))]
    for copy in few_copies:
        copy.start()
    for i in range(loads):
        load(i).start()
    beside = beside_table()
    for copy in few_copies:
        copy.wait()
    left_ref[0] = rounds_left(flagged_row[...], owner_row[...], own)
    found = arrivals(flagged_ref, owner_ref, own, me)
    for s, (mine, _, way, rank) in enumerate(found):
        place = jnp.where(mine, KEPT, EMPTY)
        for i, (c, r) in enumerate(PLACES):
            place = jnp.where(mine & (way == c) & (rank == r), i, place)
        plan_ref[s] = place
        pl.when(jnp.logical_not(mine))(put(s).start)

    diffuse = by_field(diff_ref, fields)
    courant = by_field(cour_ref, fields)
    centre = 1.0 - 6.0 * diffuse - courant
    back = diffuse + courant
    edge_ref[2] = diffuse
    edge_ref[3] = back

    def store(turn):
        span = pl.ds(pl.multiple_of(turn * CHUNK, CHUNK), CHUNK)
        return pltpu.make_async_copy(next_ref.at[span], out_ref.at[span], sem.at[turn])

    @pl.loop(0, turns)
    def _(turn):
        base = turn * CHUNK

        @pl.when(turn == 0)
        def _():
            load(0).wait()

        load(2 * turn + 1).wait()

        @pl.when(turn < turns - 1)
        def _():
            load(2 * turn + 2).wait()

        places = [(b, x) for b in range(CHUNK) for x in range(EDGE)]
        planes = [cons_ref[base + b, :, pl.ds(x * PLANE, PLANE)] for b, x in places]
        ring = dot_split(split(jnp.concatenate(planes, 0)), beside)
        low = cons_ref[jnp.maximum(base - 1, 0), :, pl.ds(CELLS - PLANE, PLANE)]
        high = cons_ref[jnp.minimum(base + CHUNK, own - 1), :, pl.ds(0, PLANE)]
        low = jnp.where(turn > 0, low, 0.0)
        high = jnp.where(turn < turns - 1, high, 0.0)
        padded = [low] + planes + [high]
        for i, (b, x) in enumerate(places):
            sides = padded[i + 2] + ring[i * fields : (i + 1) * fields]
            next_ref[base + b, :, pl.ds(x * PLANE, PLANE)] = centre * padded[i + 1] + back * padded[i] + diffuse * sides
        store(turn).start()

    for q in range(4):
        table_ref[:, pl.ds(q * PLANE, PLANE)] = refine_quarter(q)

    for s, (mine, block, way, _) in enumerate(found):
        stays = mine & (way == HOME)

        @pl.when(stays)
        def _():
            home_ref[s] = cons_ref[jnp.clip(block - me * own, 0, own - 1)]

        @pl.when(jnp.logical_not(stays))
        def _():
            home_ref[s] = jnp.zeros(home_ref.shape[1:], jnp.float32)

    edge_ref[0] = next_ref[0, :, pl.ds(0, PLANE)]
    edge_ref[1] = next_ref[own - 1, :, pl.ds(CELLS - PLANE, PLANE)]
    for turn in range(turns):
        store(turn).wait()
    for s, (mine, _, _, _) in enumerate(found):
        pl.when(jnp.logical_not(mine))(put(s).wait)


def coarse(flagged, owner, diffusivity, courant, cons):
    own, fields, cells = cons.shape
    smem = pl.BlockSpec(memory_space=pltpu.SMEM)
    vmem = pl.BlockSpec(memory_space=pltpu.VMEM)
    hbm = pl.BlockSpec(memory_space=pltpu.HBM)
    return pl.pallas_call(
        coarse_kernel,
        out_shape=[
            pltpu.HBM(cons.shape, jnp.float32),
            pltpu.HBM((CAP, 8, fields, cells), jnp.float32),
            jax.ShapeDtypeStruct((4, fields, PLANE), jnp.float32),
            jax.ShapeDtypeStruct((PLANE, 4 * PLANE), jnp.bfloat16),
            jax.ShapeDtypeStruct((CAP, fields, cells), jnp.float32),
            pltpu.SMEM((CAP,), jnp.int32),
            pltpu.SMEM((1,), jnp.int32),
        ],
        in_specs=[hbm] * 7,
        out_specs=[hbm, hbm, vmem, vmem, vmem, smem, smem],
        scratch_shapes=[
            *(pltpu.SMEM(value.shape, value.dtype) for value in (flagged, owner, diffusivity, courant)),
            pltpu.VMEM((1, flagged.shape[0]), jnp.int32),
            pltpu.VMEM((1, owner.shape[0]), jnp.int32),
            pltpu.VMEM(cons.shape, jnp.float32),
            pltpu.VMEM(cons.shape, jnp.float32),
            pltpu.VMEM((8, fields, cells), jnp.float32),
            pltpu.SemaphoreType.DMA((3 * (own // CHUNK),)),
            pltpu.SemaphoreType.DMA((6 + CAP,)),
        ],
        compiler_params=pltpu.CompilerParams(vmem_limit_bytes=20 << 20),
        cost_estimate=pl.CostEstimate(flops=2 * 2 * own * EDGE * fields * PLANE * PLANE, bytes_accessed=8 << 20, transcendentals=0),
        name="coarse",
    )(
        *(pltpu.with_memory_space_constraint(value, pltpu.HBM) for value in (flagged, owner, diffusivity, courant)),
        *(pltpu.with_memory_space_constraint(value.reshape(1, -1), pltpu.HBM) for value in (flagged, owner)),
        pltpu.with_memory_space_constraint(cons, pltpu.HBM),
    )


def collect_kernel(own, turn_ref, flagged_ref, owner_ref, *refs):
    *parts, _, home_ref = refs
    me = lax.axis_index(AXES)
    for s, (mine, _, way, rank) in enumerate(arrivals(flagged_ref, owner_ref, own, me)):
        for c, part in enumerate(parts):

            @pl.when(mine & (way == c) & (rank == room(way) + turn_ref[0]))
            def _():
                home_ref[s] = part[...]


def collect(own, turn, flagged, owner, parts, home):
    smem = pl.BlockSpec(memory_space=pltpu.SMEM)
    vmem = pl.BlockSpec(memory_space=pltpu.VMEM)
    return pl.pallas_call(
        functools.partial(collect_kernel, own),
        out_shape=jax.ShapeDtypeStruct(home.shape, jnp.float32),
        in_specs=[smem] * 3 + [vmem] * (HOME + 1),
        out_specs=vmem,
        input_output_aliases={3 + HOME: 0},
        compiler_params=pltpu.CompilerParams(vmem_limit_bytes=8 << 20),
        name="collect",
    )(turn, flagged, owner, *parts, home)


def unpack_kernel(plan_ref, *refs):
    parts, (home_ref, edge_ref, table_ref, _, _, coarse_ref, children_ref, parent_ref, child_ref, rim_ref, sem) = refs[:HOME], refs[HOME:]
    own, fields, _ = coarse_ref.shape
    me = lax.axis_index(AXES)
    def store(s, child):
        return pltpu.make_async_copy(child_ref.at[s, child], children_ref.at[s, child], sem.at[s])

    @pl.loop(0, CAP)
    def _(s):
        for i, (c, r) in enumerate([*PLACES, (None, None)]):

            @pl.when(plan_ref[s] == i)
            def _():
                parent_ref[...] = home_ref[s] if c is None else parts[c][:, pl.ds(r * CELLS, CELLS)]

        @pl.when(plan_ref[s] != EMPTY)
        def _():
            planes = [parent_ref[:, pl.ds(x * PLANE, PLANE)] for x in range(EDGE)]
            parent = split(jnp.concatenate(planes, 0))
            for q in range(4):
                fine = dot_split(parent, table_ref[:, pl.ds(q * PLANE, PLANE)])
                rows = [fine[x * fields : (x + 1) * fields] for x in range(EDGE)]
                for x in range(EDGE):
                    low, high = max(x - 1, 0), min(x + 1, EDGE - 1)
                    slope = (rows[high] - rows[low]) * (0.25 / (high - low))
                    half, place = divmod(2 * x, EDGE)
                    child_ref[s, half * 4 + q, :, pl.ds(place * PLANE, PLANE)] = rows[x] - slope
                    child_ref[s, half * 4 + q, :, pl.ds((place + 1) * PLANE, PLANE)] = rows[x] + slope
                for half in range(2):
                    store(s, half * 4 + q).start()

    rims = [parts[way][:, pl.ds(ROOM[way] * CELLS, PLANE)] for way in RIMS]
    odd = (me & 1) == 1
    rim_ref[0] = edge_ref[0] + edge_ref[3] * jnp.where(odd, rims[0], rims[1])
    rim_ref[1] = edge_ref[1] + edge_ref[2] * jnp.where(odd, rims[1], rims[0])
    spots = (coarse_ref.at[0, :, pl.ds(0, PLANE)], coarse_ref.at[own - 1, :, pl.ds(CELLS - PLANE, PLANE)])
    ends = [pltpu.make_async_copy(rim_ref.at[c], spots[c], sem.at[CAP + c]) for c in range(2)]
    for copy in ends:
        copy.start()

    for s in range(CAP):
        pl.when(plan_ref[s] != EMPTY)(pltpu.make_async_copy(child_ref.at[s], children_ref.at[s], sem.at[s]).wait)

    for copy in ends:
        copy.wait()


def unpack(plan, parts, home, edges, table, stepped, children):
    fields = stepped.shape[1]
    vmem = pl.BlockSpec(memory_space=pltpu.VMEM)
    hbm = pl.BlockSpec(memory_space=pltpu.HBM)
    family = pltpu.HBM((CAP, 8, fields, CELLS), jnp.float32)
    return pl.pallas_call(
        unpack_kernel,
        out_shape=[pltpu.HBM(stepped.shape, jnp.float32), family],
        in_specs=[pl.BlockSpec(memory_space=pltpu.SMEM)] + [vmem] * (HOME + 3) + [hbm, hbm],
        out_specs=[hbm, hbm],
        scratch_shapes=[
            pltpu.VMEM((fields, CELLS), jnp.float32),
            pltpu.VMEM(family.shape, jnp.float32),
            pltpu.VMEM((2, fields, PLANE), jnp.float32),
            pltpu.SemaphoreType.DMA((CAP + 2,)),
        ],
        input_output_aliases={HOME + 4: 0, HOME + 5: 1},
        compiler_params=pltpu.CompilerParams(vmem_limit_bytes=24 << 20),
        cost_estimate=pl.CostEstimate(flops=2 * 2 * CAP * EDGE * fields * PLANE * 4 * PLANE, bytes_accessed=5 << 20, transcendentals=0),
        name="unpack",
    )(plan, *parts, home, edges, table, stepped, children)


def shards(cons_old, flagged, new_owner, diffusivity, courant):
    own = cons_old.shape[0]
    arrived = exchange(pack(flagged, new_owner, cons_old))
    stepped, children, edges, table, home, plan, left = coarse(flagged, new_owner, diffusivity, courant, cons_old)
    left = left.reshape(())

    def later(carry):
        turn, home = carry
        at = turn.reshape((1,))
        parts = exchange(pack(flagged, new_owner, cons_old, at))
        return turn + 1, collect(own, at, flagged, new_owner, parts, home)

    home, arrived = lax.optimization_barrier((home, arrived))
    _, home = lax.while_loop(lambda carry: carry[0] < left, later, (jnp.int32(0), home))
    return tuple(unpack(plan, arrived, home, edges, table, stepped, children))


def solution(mesh):
    in_specs = (P(AXES, None, None), P(), P(), P(), P())
    out_specs = (P(AXES, None, None), P(AXES, None, None, None))
    return jax.shard_map(shards, mesh=mesh, in_specs=in_specs, out_specs=out_specs, check_vma=False)
```
